512 devices in a mesh: src: 32 (over z, x), tile: 16 (over y, core).
Axes of the slice: x: 4, y: 8, z: 8, core: 2. Of those that a mesh axis runs over, the one named last changes fastest.
Arguments:
- spectra: bfloat16 [32, 2, 128, 128], P('tile'), may hold values from -0.06 to 0.06
- pupils: bfloat16 [16, 128, 2, 128, 128], P('tile', 'src'), may hold values from -6 to 6
- zone_of: int32 [32], replicated, may hold values from 0 to 15
- density: int32 [32], replicated, may hold values from 1 to 4
- assignment: int32 [32], replicated, may hold values from 0 to 31, each once
- weights: int32 [128], P('src'), may hold values from 1 to 16
Outputs:
- intensity: float32 [128, 32, 2048], P('src', 'tile')
The draws below stay inside these ranges and needn't reach their ends.
Inputs may be any that keep to these rules, and one draw needn't show every extreme that they name: `assignment`: a permutation of the tiles.
All inputs are finite; a program needn't handle non-finite values.
Results may differ from the reference program's by a relative error of at most 0.0018.
Values may be sent and summed in bfloat16 or wider, within the bound.
No kernel may reach another device: no remote copies, remote signals or barrier semaphores. Data moves between devices by JAX's collectives and lax.ppermute only.
A program may use at most 64 MiB of HBM per device.

```python
import math
import jax
import jax.numpy as jnp
from jax import lax

K = 128
NPIX = 2048
ROWS = 128
SOURCES = 128
TILES = 32
ZONES = 16


def draw_spectra(key, part):
    key = jax.random.fold_in(key, 11)
    freq = jnp.arange(K, dtype=jnp.int32) - K // 2
    band = K // 8
    edge = jnp.mod(jnp.abs(freq), band) >= band - 2
    row_scale = jnp.where(edge, 1.0, 0.05).astype(jnp.float32)[None, None, :, None]
    values = jnp.clip(0.025 * jax.random.normal(key, (TILES, 2, K, K), jnp.float32), -0.0598, 0.0598)
    return (values * row_scale).astype(jnp.bfloat16)


def place_ends(drawn, rng, low, largest):
    place = [jax.random.randint(jax.random.fold_in(rng, axis), (), 0, length) for axis, length in enumerate(drawn.shape)]
    widest = drawn.shape.index(max(drawn.shape))
    next_to = place[:widest] + [(place[widest] + 1) % drawn.shape[widest]] + place[widest + 1:]
    return drawn.at[tuple(place)].set(low).at[tuple(next_to)].set(largest)


def steps_of(rng, extent, pieces, least, largest):
    factor_of = 1.0
    for dim, parts in pieces:
        draws = jax.random.uniform(jax.random.fold_in(jax.random.fold_in(rng, 6), dim), (parts,), jnp.float32, least / len(pieces), largest / len(pieces))
        factor_of = factor_of * jnp.repeat(jnp.exp(draws), extent[dim] // parts).reshape((-1,) + (1,) * (len(extent) - 1 - dim))
    return factor_of


def gaussian(stream_key, shape, width, reach, pieces=(), kind=jnp.bfloat16):
    drawn = jax.random.normal(stream_key, shape, jnp.float32) * width
    if len(pieces) > 0:
        drawn = steps_of(stream_key, shape, pieces, -0.22, 0.18) * drawn
    return jnp.clip(drawn, min=-reach, max=reach).astype(kind)


def setup_inputs(seed: int = 0) -> dict:
    seeds = jax.random.split(jax.random.key(seed), 7)
    return {
        "spectra": draw_spectra(jax.random.fold_in(seeds[6], 71), 0),
        "pupils": gaussian(seeds[1], (ZONES, SOURCES, 2, K, K), 1.0, 6.0, ((0, 16), (1, 32))),
        "zone_of": place_ends(jax.random.randint(seeds[2], (TILES,), 0, ZONES), jax.random.fold_in(seeds[2], 1), 0, ZONES - 1).astype(jnp.int32),
        "density": place_ends(jax.random.randint(seeds[3], (TILES,), 1, 5), jax.random.fold_in(seeds[3], 1), 1, 4).astype(jnp.int32),
        "assignment": jax.random.permutation(seeds[4], TILES).astype(jnp.int32),
        "weights": place_ends(jax.random.randint(seeds[5], (SOURCES,), 1, 17), jax.random.fold_in(seeds[5], 1), 1, 16).astype(jnp.int32),
    }


def tables(freq_count, pixels, row_count):
    freq = jnp.arange(freq_count, dtype=jnp.int32) - freq_count // 2
    cols = jnp.arange(pixels, dtype=jnp.int32)
    angle = jnp.mod(freq[:, None] * cols[None, :], pixels).astype(jnp.float32) * (2.0 * math.pi / pixels)
    col_cos = jnp.cos(angle)
    col_sin = jnp.sin(angle)
    col_mat = jnp.concatenate([jnp.concatenate([col_cos, col_sin], 1), jnp.concatenate([-col_sin, col_cos], 1)], 0).astype(jnp.bfloat16)
    rws = jnp.arange(row_count, dtype=jnp.int32)
    phase = jnp.mod(rws[:, None] * freq[None, :], pixels).astype(jnp.float32) * (2.0 * math.pi / pixels)
    row_mat = jnp.concatenate([jnp.cos(phase), jnp.sin(phase)], 1).astype(jnp.bfloat16)
    return col_mat, row_mat


def half_field(pupil, spectrum, keep, col_mat):
    pupil_re = pupil[0].astype(jnp.float32)
    pupil_im = pupil[1].astype(jnp.float32)
    mask_re = spectrum[0].astype(jnp.float32)
    mask_im = spectrum[1].astype(jnp.float32)
    prod_re = (pupil_re * mask_re - pupil_im * mask_im) * keep
    prod_im = (pupil_re * mask_im + pupil_im * mask_re) * keep
    stacked = jnp.concatenate([prod_re, prod_im], 1).astype(jnp.bfloat16)
    return jnp.dot(stacked, col_mat, preferred_element_type=jnp.float32).astype(jnp.bfloat16)


def image_power(half, row_mat):
    pixels = half.shape[1] // 2
    half_re = half[:, :pixels]
    half_im = half[:, pixels:]
    second = jnp.concatenate([half, jnp.concatenate([-half_im, half_re], 1)], 0)
    field = jnp.dot(row_mat, second, preferred_element_type=jnp.float32)
    return field[:, :pixels] * field[:, :pixels] + field[:, pixels:] * field[:, pixels:]


def reference(spectra, pupils, zone_of, density, assignment, weights):
    col_mat, row_mat = tables(K, NPIX, ROWS)
    weight_f = weights.astype(jnp.float32)
    total = jnp.sum(weight_f)
    freq = jnp.arange(K, dtype=jnp.int32) - K // 2

    def one_slot(tile):
        zone = zone_of[tile]
        level = density[tile]
        keep = (jnp.abs(freq) * 8 < level * K).astype(jnp.float32)[:, None]
        spectrum = spectra[tile]

        def add_source(accum, source):
            half = half_field(pupils[zone, source], spectrum, keep, col_mat)
            return accum + weight_f[source] * image_power(half, row_mat), None

        accum, _ = lax.scan(add_source, jnp.zeros((ROWS, NPIX), jnp.float32), jnp.arange(SOURCES, dtype=jnp.int32))
        return accum / total

    images = lax.map(one_slot, assignment)
    return jnp.transpose(images, (1, 0, 2))
```

```python
import math

import jax
import jax.numpy as jnp
import ml_dtypes
import numpy as np
from jax import lax
from jax.experimental import pallas as pl
from jax.experimental.pallas import tpu as pltpu
from jax.sharding import PartitionSpec as P

K = 128
NPIX = 2048
ROWS = 128
SAMPLES = 255
WIDE = 256
VMEM_LIMIT = 48 * 1024 * 1024


def sample_table():
    freq = np.arange(K) - K // 2
    point = np.arange(SAMPLES)
    angle = np.mod(freq[:, None] * point[None, :], SAMPLES) * (2.0 * math.pi / SAMPLES)
    table = np.zeros((K, 2 * WIDE))
    table[:, :SAMPLES] = np.cos(angle)
    table[:, WIDE : WIDE + SAMPLES] = np.sin(angle)
    return table.astype(ml_dtypes.bfloat16)


def row_tables(blocks):
    freq = np.arange(K) - K // 2
    place = np.arange(ROWS)
    group, lane = place // 8, place % 8
    even = lane % 2 == 0
    first = np.where(even, 8 * group + lane // 2, 8 * group + 4 + lane // 2)
    second = np.where(even, 8 * group + 4 + lane // 2, 8 * group + lane // 2)
    out = []
    for order in (first, second):
        phase = np.mod(order[:, None] * freq[None, :], NPIX) * (2.0 * math.pi / NPIX)
        both = np.stack([np.cos(phase), np.sin(phase)], 1).reshape(ROWS, 2, blocks, K // blocks)
        out.append(both.transpose(0, 2, 1, 3).reshape(ROWS, 2 * K))
    return np.stack(out).astype(ml_dtypes.bfloat16)


def interpolation_table():
    theta = 2.0 * math.pi * (np.arange(NPIX)[None, :] / NPIX - np.arange(SAMPLES)[:, None] / SAMPLES)
    half = np.sin(theta / 2)
    safe = np.where(np.abs(half) < 1e-12, 1.0, half)
    kernel = np.where(np.abs(half) < 1e-12, 1.0, np.sin(SAMPLES * theta / 2) / (SAMPLES * safe))
    table = np.zeros((WIDE, NPIX))
    table[:SAMPLES] = kernel
    high = table.astype(ml_dtypes.bfloat16)
    low = (table - high.astype(np.float64)).astype(ml_dtypes.bfloat16)
    return high, low


def product_kernel(assignment, zone_of, density, index, held, out):
    slots = assignment.shape[0]
    per_device = slots // out.shape[0]
    sources = 4
    freq = lax.broadcasted_iota(jnp.int32, (8, K), 0) + index[0] * 8 - K // 2
    distance = jnp.abs(freq) * 8
    for slot in range(slots):
        tile = assignment[slot]
        zone = zone_of[tile]
        keep = (distance < density[tile] * K).astype(jnp.float32)
        pupil = held[zone, 0:64, :].astype(jnp.float32).reshape(sources, 2, 8, K)
        start = pl.multiple_of(64 + 16 * (tile % 2), 16)
        mask = held[tile // 2, pl.ds(start, 16), :].astype(jnp.float32).reshape(2, 8, K)
        real = (pupil[:, 0] * mask[0] - pupil[:, 1] * mask[1]) * keep
        imag = (pupil[:, 0] * mask[1] + pupil[:, 1] * mask[0]) * keep
        both = jnp.stack([real, imag], 1).reshape(64, K).astype(jnp.bfloat16)
        out[slot // per_device, 64 * (slot % per_device) : 64 * (slot % per_device) + 64, :] = both


def image_kernel(weights, products, columns, rows, out):
    sources = 4
    blocks = products.shape[0]
    table = columns[...]
    images = []
    for slot in range(2):
        total = jnp.zeros((ROWS, WIDE), jnp.float32)
        for source in range(sources):
            start = (slot * sources + source) * 16
            product = products[:, start : start + 16, :].reshape(blocks * 16, K)
            half = jnp.dot(product, table, preferred_element_type=jnp.float32)
            half = half.reshape(blocks, 2, 8, 2 * WIDE)
            real = half[:, 0, :, :WIDE] - half[:, 1, :, WIDE:]
            imag = half[:, 0, :, WIDE:] + half[:, 1, :, :WIDE]
            upper = jnp.concatenate([real, imag], -1)
            lower = jnp.concatenate([-imag, real], -1)
            second = jnp.stack([upper, lower], 1).reshape(2 * K, 2 * WIDE).astype(jnp.bfloat16)
            field = jnp.dot(rows[slot], second, preferred_element_type=jnp.float32)
            power = field[:, :WIDE] * field[:, :WIDE] + field[:, WIDE:] * field[:, WIDE:]
            total = total + weights[source].astype(jnp.float32) * power
        images.append(total)
    weight_sum = weights[0] + weights[1] + weights[2] + weights[3]
    last = lax.broadcasted_iota(jnp.int32, (ROWS, WIDE), 1) == SAMPLES
    even = lax.broadcasted_iota(jnp.int32, (ROWS, WIDE), 0) % 2 == 0
    first = jnp.where(last, weight_sum.astype(jnp.float32), images[0])
    second = jnp.where(last, weight_sum.astype(jnp.float32), images[1])
    lower = jnp.where(even, first, second).reshape(ROWS // 8, 8, WIDE)
    upper = jnp.where(even, pltpu.roll(first, ROWS - 1, 0), pltpu.roll(second, 1, 0)).reshape(ROWS // 8, 8, WIDE)
    out[...] = jnp.stack([lower, upper], 1).reshape(ROWS // 4, 8, WIDE)


def finish_kernel(parts, high, low, out):
    summed = jnp.sum(parts[...], 0)
    total = summed[:, SAMPLES:]
    coarse = summed.astype(jnp.bfloat16)
    fine = (summed - coarse.astype(jnp.float32)).astype(jnp.bfloat16)
    both = jnp.concatenate([coarse, fine], 0)
    by_high = jnp.dot(both, high[...], preferred_element_type=jnp.float32)
    by_low = jnp.dot(coarse, low[...], preferred_element_type=jnp.float32)
    result = (by_high[:8] + by_high[8:] + by_low) / total
    out[...] = result


def shards(spectra, pupils, zone_of, density, assignment, weights):
    devices = lax.axis_size("tile")
    sources = pupils.shape[1]
    scalars = pl.BlockSpec(memory_space=pltpu.SMEM)
    blocks = pl.BlockSpec(memory_space=pltpu.VMEM)
    params = pltpu.CompilerParams(vmem_limit_bytes=VMEM_LIMIT)

    pupil_rows = pupils[0].reshape(sources, 2, devices, 8, K).transpose(2, 0, 1, 3, 4).reshape(devices, sources * 16, K)
    mask_rows = spectra.reshape(2, 2, devices, 8, K).transpose(2, 0, 1, 3, 4).reshape(devices, 32, K)
    held = lax.all_to_all(jnp.concatenate([pupil_rows, mask_rows], 1), "tile", 0, 0, tiled=True)

    index = lax.axis_index("tile").astype(jnp.int32).reshape(1)
    products = pl.pallas_call(
        product_kernel,
        out_shape=jax.ShapeDtypeStruct((devices, 2 * sources * 16, K), jnp.bfloat16),
        in_specs=[scalars] * 4 + [blocks],
        out_specs=blocks,
        compiler_params=params,
        name="products",
    )(assignment, zone_of, density, index, held)
    products = lax.all_to_all(products, "tile", 0, 0, tiled=True)

    image = pl.pallas_call(
        image_kernel,
        out_shape=jax.ShapeDtypeStruct((ROWS // 4, 8, WIDE), jnp.float32),
        in_specs=[scalars] + [blocks] * 3,
        out_specs=blocks,
        compiler_params=params,
        name="images",
    )(weights, products, jnp.asarray(sample_table()), jnp.asarray(row_tables(devices)))
    parts = lax.all_to_all(image, "src", 0, 0, tiled=True)

    high, low = interpolation_table()
    result = pl.pallas_call(
        finish_kernel,
        out_shape=jax.ShapeDtypeStruct((8, NPIX), jnp.float32),
        in_specs=[blocks] * 3,
        out_specs=blocks,
        compiler_params=params,
        name="finish",
    )(parts, jnp.asarray(high), jnp.asarray(low))
    return result.reshape(4, 2, NPIX)


def solution(mesh):
    return jax.shard_map(
        shards,
        mesh=mesh,
        in_specs=(
            P("tile", None, None, None),
            P("tile", "src", None, None, None),
            P(),
            P(),
            P(),
            P("src"),
        ),
        out_specs=P("src", "tile", None),
        check_vma=False,
    )
```

```python
import math

import jax
import jax.numpy as jnp
import ml_dtypes
import numpy as np
from jax import lax
from jax.experimental import pallas as pl
from jax.experimental.pallas import tpu as pltpu
from jax.sharding import PartitionSpec as P

K = 128
NPIX = 2048
ROWS = 128
SAMPLES = 255
WIDE = 256
VMEM_LIMIT = 48 * 1024 * 1024


def sample_table():
    freq = np.arange(K) - K // 2
    point = np.arange(SAMPLES)
    angle = np.mod(freq[:, None] * point[None, :], SAMPLES) * (2.0 * math.pi / SAMPLES)
    table = np.zeros((2, K, 2, WIDE))
    table[0, :, 0, :SAMPLES] = np.cos(angle)
    table[0, :, 1, :SAMPLES] = np.sin(angle)
    table[1, :, 0, :SAMPLES] = -np.sin(angle)
    table[1, :, 1, :SAMPLES] = np.cos(angle)
    return table.reshape(2 * K, 2 * WIDE).astype(ml_dtypes.bfloat16)


def row_tables():
    freq = np.arange(K) - K // 2
    place = np.arange(ROWS)
    group, lane = place // 8, place % 8
    even = lane % 2 == 0
    first = np.where(even, 8 * group + lane // 2, 8 * group + 4 + lane // 2)
    second = np.where(even, 8 * group + 4 + lane // 2, 8 * group + lane // 2)
    out = []
    for order in (first, second):
        phase = np.mod(order[:, None] * freq[None, :], NPIX) * (2.0 * math.pi / NPIX)
        out.append(np.concatenate([np.cos(phase), np.sin(phase)], 1))
    return np.stack(out).astype(ml_dtypes.bfloat16)


def interpolation_table():
    theta = 2.0 * math.pi * (np.arange(NPIX)[None, :] / NPIX - np.arange(SAMPLES)[:, None] / SAMPLES)
    half = np.sin(theta / 2)
    safe = np.where(np.abs(half) < 1e-12, 1.0, half)
    kernel = np.where(np.abs(half) < 1e-12, 1.0, np.sin(SAMPLES * theta / 2) / (SAMPLES * safe))
    table = np.zeros((WIDE, NPIX))
    table[:SAMPLES] = kernel
    high = table.astype(ml_dtypes.bfloat16)
    low = (table - high.astype(np.float64)).astype(ml_dtypes.bfloat16)
    return high, low


def layout_kernel(pupils, spectra, out, done):
    copies = []
    for piece in range(12):
        source = pupils.at[piece // 2, piece % 2] if piece < 8 else spectra.at[(piece - 8) // 2, piece % 2]
        copies.append(pltpu.make_async_copy(source, out.at[:, piece], done.at[piece]))
    for copy in copies:
        copy.start()
    for copy in copies:
        copy.wait()


def product_kernel(assignment, zone_of, density, index, held, out):
    slots = assignment.shape[0]
    per_device = slots // out.shape[0]
    sources = 4
    freq = lax.broadcasted_iota(jnp.int32, (8, K), 0) + index[0] * 8 - K // 2
    distance = jnp.abs(freq) * 8
    for slot in range(slots):
        tile = assignment[slot]
        zone = zone_of[tile]
        keep = (distance < density[tile] * K).astype(jnp.float32)
        pupil = held[zone, 0:64, :].astype(jnp.float32).reshape(sources, 2, 8, K)
        start = pl.multiple_of(64 + 16 * (tile % 2), 16)
        mask = held[tile // 2, pl.ds(start, 16), :].astype(jnp.float32).reshape(2, 8, K) * keep
        real = pupil[:, 0] * mask[0] - pupil[:, 1] * mask[1]
        imag = pupil[:, 0] * mask[1] + pupil[:, 1] * mask[0]
        both = jnp.stack([real.reshape(2, 16, K), imag.reshape(2, 16, K)], 1).reshape(64, K)
        first = 64 * (slot % per_device)
        out[slot // per_device, first : first + 64, :] = both.astype(jnp.bfloat16)


def image_kernel(weights, products, columns, rows, out):
    table = columns[...]
    images = []
    for slot in range(2):
        total = jnp.zeros((ROWS, WIDE), jnp.float32)
        for pair in range(2):
            start = (slot * 2 + pair) * 32
            real = products[:, start : start + 16, :].reshape(2 * K, K)
            imag = products[:, start + 16 : start + 32, :].reshape(2 * K, K)
            halves = jnp.dot(jnp.concatenate([real, imag], 1), table, preferred_element_type=jnp.float32)
            halves = halves.reshape(K // 8, 2, 8, 2 * WIDE)
            for source in range(2):
                half = halves[:, source].reshape(K, 2 * WIDE)
                crossed = jnp.concatenate([-half[:, WIDE:], half[:, :WIDE]], 1)
                second = jnp.concatenate([half.astype(jnp.bfloat16), crossed.astype(jnp.bfloat16)], 0)
                field = jnp.dot(rows[slot], second, preferred_element_type=jnp.float32)
                power = field[:, :WIDE] * field[:, :WIDE] + field[:, WIDE:] * field[:, WIDE:]
                total = total + weights[pair * 2 + source].astype(jnp.float32) * power
        images.append(total)
    weight_sum = weights[0] + weights[1] + weights[2] + weights[3]
    last = lax.broadcasted_iota(jnp.int32, (ROWS, WIDE), 1) == SAMPLES
    even = lax.broadcasted_iota(jnp.int32, (ROWS, WIDE), 0) % 2 == 0
    first = jnp.where(last, weight_sum.astype(jnp.float32), images[0])
    second = jnp.where(last, weight_sum.astype(jnp.float32), images[1])
    lower = jnp.where(even, first, second).reshape(ROWS // 8, 8, WIDE)
    upper = jnp.where(even, pltpu.roll(first, ROWS - 1, 0), pltpu.roll(second, 1, 0)).reshape(ROWS // 8, 8, WIDE)
    out[...] = jnp.stack([lower, upper], 1).reshape(ROWS // 4, 8, WIDE).astype(out.dtype)


def finish_kernel(parts, high, low, out):
    summed = jnp.sum(parts[...].astype(jnp.float32), 0)
    total = summed[:, SAMPLES:]
    coarse = summed.astype(jnp.bfloat16)
    fine = (summed - coarse.astype(jnp.float32)).astype(jnp.bfloat16)
    both = jnp.concatenate([coarse, fine], 0)
    by_high = jnp.dot(both, high[...], preferred_element_type=jnp.float32)
    by_low = jnp.dot(coarse, low[...], preferred_element_type=jnp.float32)
    result = (by_high[:8] + by_high[8:] + by_low) / total
    for row in range(out.shape[0]):
        out[row] = result[2 * row : 2 * row + 2]


def shards(spectra, pupils, zone_of, density, assignment, weights):
    devices = lax.axis_size("tile")
    sources = pupils.shape[1]
    scalars = pl.BlockSpec(memory_space=pltpu.SMEM)
    blocks = pl.BlockSpec(memory_space=pltpu.VMEM)
    params = pltpu.CompilerParams(vmem_limit_bytes=VMEM_LIMIT)

    hbm = pl.BlockSpec(memory_space=pltpu.HBM)
    laid = pl.pallas_call(
        layout_kernel,
        out_shape=jax.ShapeDtypeStruct((devices, 12, 8, K), jnp.bfloat16),
        in_specs=[hbm, hbm],
        out_specs=blocks,
        scratch_shapes=[pltpu.SemaphoreType.DMA((12,))],
        compiler_params=params,
        name="layout",
    )(pupils.reshape(sources, 2, devices, 8, K), spectra.reshape(2, 2, devices, 8, K))
    held = lax.all_to_all(laid.reshape(devices, 96, K), "tile", 0, 0, tiled=True)

    index = lax.axis_index("tile").astype(jnp.int32).reshape(1)
    products = pl.pallas_call(
        product_kernel,
        out_shape=jax.ShapeDtypeStruct((devices, 2 * sources * 16, K), jnp.bfloat16),
        in_specs=[scalars] * 4 + [blocks],
        out_specs=blocks,
        compiler_params=params,
        name="products",
    )(assignment, zone_of, density, index, held)
    products = lax.all_to_all(products, "tile", 0, 0, tiled=True)

    image = pl.pallas_call(
        image_kernel,
        out_shape=jax.ShapeDtypeStruct((ROWS // 4, 8, WIDE), jnp.bfloat16),
        in_specs=[scalars] + [blocks] * 3,
        out_specs=blocks,
        compiler_params=params,
        name="images",
    )(weights, products, jnp.asarray(sample_table()), jnp.asarray(row_tables()))
    parts = lax.all_to_all(image, "src", 0, 0, tiled=True)

    high, low = interpolation_table()
    return pl.pallas_call(
        finish_kernel,
        out_shape=jax.ShapeDtypeStruct((4, 2, NPIX), jnp.float32),
        in_specs=[blocks] * 3,
        out_specs=blocks,
        compiler_params=params,
        name="finish",
    )(parts, jnp.asarray(high), jnp.asarray(low))


def solution(mesh):
    return jax.shard_map(
        shards,
        mesh=mesh,
        in_specs=(
            P("tile", None, None, None),
            P("tile", "src", None, None, None),
            P(),
            P(),
            P(),
            P("src"),
        ),
        out_specs=P("src", "tile", None),
        check_vma=False,
    )
```

```python
import math

import jax
import jax.numpy as jnp
import ml_dtypes
import numpy as np
from jax import lax
from jax.experimental import pallas as pl
from jax.experimental.pallas import tpu as pltpu
from jax.sharding import PartitionSpec as P

K = 128
NPIX = 2048
ROWS = 128
SAMPLES = 255
WIDE = 256
VMEM_LIMIT = 48 * 1024 * 1024


def sample_table():
    freq = np.arange(K) - K // 2
    point = np.arange(SAMPLES)
    angle = np.mod(freq[:, None] * point[None, :], SAMPLES) * (2.0 * math.pi / SAMPLES)
    table = np.zeros((2, K, 2, WIDE))
    table[0, :, 0, :SAMPLES] = np.cos(angle)
    table[0, :, 1, :SAMPLES] = np.sin(angle)
    table[1, :, 0, :SAMPLES] = -np.sin(angle)
    table[1, :, 1, :SAMPLES] = np.cos(angle)
    return table.reshape(2 * K, 2 * WIDE).astype(ml_dtypes.bfloat16)


def row_tables():
    freq = np.arange(K) - K // 2
    place = np.arange(ROWS)
    group, lane = place // 8, place % 8
    even = lane % 2 == 0
    first = np.where(even, 8 * group + lane // 2, 8 * group + 4 + lane // 2)
    second = np.where(even, 8 * group + 4 + lane // 2, 8 * group + lane // 2)
    out = []
    for order in (first, second):
        phase = np.mod(order[:, None] * freq[None, :], NPIX) * (2.0 * math.pi / NPIX)
        cos, sin = np.cos(phase), np.sin(phase)
        out.append(np.block([[cos, -sin], [sin, cos]]))
    return np.stack(out).astype(ml_dtypes.bfloat16)


def interpolation_table():
    theta = 2.0 * math.pi * (np.arange(NPIX)[None, :] / NPIX - np.arange(SAMPLES)[:, None] / SAMPLES)
    half = np.sin(theta / 2)
    safe = np.where(np.abs(half) < 1e-12, 1.0, half)
    kernel = np.where(np.abs(half) < 1e-12, 1.0, np.sin(SAMPLES * theta / 2) / (SAMPLES * safe))
    table = np.zeros((WIDE, NPIX))
    table[:SAMPLES] = kernel
    high = table.astype(ml_dtypes.bfloat16)
    low = (table - high.astype(np.float64)).astype(ml_dtypes.bfloat16)
    return high, low


def layout_kernel(pupils, spectra, out, done):
    copies = []
    for piece in range(12):
        source = pupils.at[piece // 2, piece % 2] if piece < 8 else spectra.at[(piece - 8) // 2, piece % 2]
        copies.append(pltpu.make_async_copy(source, out.at[:, piece], done.at[piece]))
    for copy in copies:
        copy.start()
    for copy in copies:
        copy.wait()


def product_kernel(assignment, zone_of, density, held, out):
    slots = assignment.shape[0]
    per_device = slots // out.shape[0]
    sources = 4
    freq = lax.broadcasted_iota(jnp.int32, (8, K), 0) + lax.axis_index("tile") * 8 - K // 2
    distance = jnp.abs(freq) * 8
    for slot in range(slots):
        tile = assignment[slot]
        zone = zone_of[tile]
        keep = (distance < density[tile] * K).astype(jnp.float32)
        pupil = held[zone, 0:64, :].astype(jnp.float32).reshape(sources, 2, 8, K)
        start = pl.multiple_of(64 + 16 * (tile % 2), 16)
        mask = held[tile // 2, pl.ds(start, 16), :].astype(jnp.float32).reshape(2, 8, K) * keep
        real = pupil[:, 0] * mask[0] - pupil[:, 1] * mask[1]
        imag = pupil[:, 0] * mask[1] + pupil[:, 1] * mask[0]
        both = jnp.stack([real.reshape(2, 16, K), imag.reshape(2, 16, K)], 1).reshape(64, K)
        first = 64 * (slot % per_device)
        out[slot // per_device, first : first + 64, :] = both.astype(jnp.bfloat16)


def image_kernel(weights, products, columns, rows, out):
    stacked = []
    for piece in range(4):
        real = products[:, 32 * piece : 32 * piece + 16, :].reshape(2 * K, K)
        imag = products[:, 32 * piece + 16 : 32 * piece + 32, :].reshape(2 * K, K)
        stacked.append(jnp.concatenate([real, imag], 1))
    halves = jnp.dot(jnp.concatenate(stacked, 0), columns[...], preferred_element_type=jnp.float32)
    halves = halves.reshape(2, 2, K // 8, 2, 8, 2 * WIDE)
    images = []
    for slot in range(2):
        sides = []
        for source in range(4):
            half = halves[slot, source // 2, :, source % 2].reshape(K, 2 * WIDE).astype(jnp.bfloat16)
            sides.append(jnp.concatenate([half[:, :WIDE], half[:, WIDE:]], 0))
        field = jnp.dot(rows[slot], jnp.concatenate(sides, 1), preferred_element_type=jnp.float32)
        power = field[:ROWS] * field[:ROWS] + field[ROWS:] * field[ROWS:]
        total = jnp.zeros((ROWS, WIDE), jnp.float32)
        for source in range(4):
            total = total + weights[source].astype(jnp.float32) * power[:, source * WIDE : (source + 1) * WIDE]
        images.append(total)
    weight_sum = weights[0] + weights[1] + weights[2] + weights[3]
    last = lax.broadcasted_iota(jnp.int32, (ROWS, WIDE), 1) == SAMPLES
    even = lax.broadcasted_iota(jnp.int32, (ROWS, WIDE), 0) % 2 == 0
    first = jnp.where(last, weight_sum.astype(jnp.float32), images[0])
    second = jnp.where(last, weight_sum.astype(jnp.float32), images[1])
    lower = jnp.where(even, first, second).reshape(ROWS // 8, 8, WIDE)
    upper = jnp.where(even, pltpu.roll(first, ROWS - 1, 0), pltpu.roll(second, 1, 0)).reshape(ROWS // 8, 8, WIDE)
    out[...] = jnp.stack([lower, upper], 1).reshape(ROWS // 4, 8, WIDE).astype(out.dtype)


def finish_kernel(parts, high, low, out, held, done):
    summed = jnp.sum(parts[...].astype(jnp.float32), 0)
    total = summed[:, SAMPLES:]
    coarse = summed.astype(jnp.bfloat16)
    fine = (summed - coarse.astype(jnp.float32)).astype(jnp.bfloat16)
    both = jnp.concatenate([coarse, fine], 0)
    copies = []
    width = NPIX // 4
    for piece in range(4):
        cut = pl.ds(width * piece, width)
        by_high = jnp.dot(both, high[:, cut], preferred_element_type=jnp.float32)
        by_low = jnp.dot(coarse, low[:, cut], preferred_element_type=jnp.float32)
        result = (by_high[:8] + by_high[8:] + by_low) / total
        for row in range(4):
            held[row, :, cut] = result[2 * row : 2 * row + 2]
        copy = pltpu.make_async_copy(held.at[:, :, cut], out.at[:, :, cut], done.at[piece])
        copy.start()
        copies.append(copy)
    for copy in copies:
        copy.wait()


def shards(spectra, pupils, zone_of, density, assignment, weights):
    devices = lax.axis_size("tile")
    sources = pupils.shape[1]
    scalars = pl.BlockSpec(memory_space=pltpu.SMEM)
    blocks = pl.BlockSpec(memory_space=pltpu.VMEM)
    params = pltpu.CompilerParams(vmem_limit_bytes=VMEM_LIMIT)

    hbm = pl.BlockSpec(memory_space=pltpu.HBM)
    laid = pl.pallas_call(
        layout_kernel,
        out_shape=jax.ShapeDtypeStruct((devices, 12, 8, K), jnp.bfloat16),
        in_specs=[hbm, hbm],
        out_specs=blocks,
        scratch_shapes=[pltpu.SemaphoreType.DMA((12,))],
        name="layout",
    )(pupils.reshape(sources, 2, devices, 8, K), spectra.reshape(2, 2, devices, 8, K))
    held = lax.all_to_all(laid.reshape(devices, 96, K), "tile", 0, 0, tiled=True)

    products = pl.pallas_call(
        product_kernel,
        out_shape=jax.ShapeDtypeStruct((devices, 2 * sources * 16, K), jnp.bfloat16),
        in_specs=[scalars] * 3 + [blocks],
        out_specs=blocks,
        compiler_params=params,
        name="products",
    )(assignment, zone_of, density, held)
    products = lax.all_to_all(products, "tile", 0, 0, tiled=True)

    image = pl.pallas_call(
        image_kernel,
        out_shape=jax.ShapeDtypeStruct((ROWS // 4, 8, WIDE), jnp.bfloat16),
        in_specs=[scalars] + [blocks] * 3,
        out_specs=blocks,
        compiler_params=params,
        name="images",
    )(weights, products, jnp.asarray(sample_table()), jnp.asarray(row_tables()))
    parts = lax.all_to_all(image, "src", 0, 0, tiled=True)

    high, low = interpolation_table()
    return pl.pallas_call(
        finish_kernel,
        out_shape=jax.ShapeDtypeStruct((4, 2, NPIX), jnp.float32),
        in_specs=[blocks] * 3,
        out_specs=hbm,
        scratch_shapes=[pltpu.VMEM((4, 2, NPIX), jnp.float32), pltpu.SemaphoreType.DMA((4,))],
        compiler_params=params,
        name="finish",
    )(parts, jnp.asarray(high), jnp.asarray(low))


def solution(mesh):
    return jax.shard_map(
        shards,
        mesh=mesh,
        in_specs=(
            P("tile", None, None, None),
            P("tile", "src", None, None, None),
            P(),
            P(),
            P(),
            P("src"),
        ),
        out_specs=P("src", "tile", None),
        check_vma=False,
    )
```

```python
import math

import jax
import jax.numpy as jnp
import ml_dtypes
import numpy as np
from jax import lax
from jax.experimental import pallas as pl
from jax.experimental.pallas import tpu as pltpu
from jax.sharding import PartitionSpec as P

K = 128
NPIX = 2048
ROWS = 128
SAMPLES = 255
WIDE = 256
VMEM_LIMIT = 48 * 1024 * 1024


def sample_table():
    freq = np.arange(K) - K // 2
    point = np.arange(SAMPLES)
    angle = np.mod(freq[:, None] * point[None, :], SAMPLES) * (2.0 * math.pi / SAMPLES)
    table = np.zeros((2, K, 2, WIDE))
    table[0, :, 0, :SAMPLES] = np.cos(angle)
    table[0, :, 1, :SAMPLES] = np.sin(angle)
    table[1, :, 0, :SAMPLES] = -np.sin(angle)
    table[1, :, 1, :SAMPLES] = np.cos(angle)
    return table.reshape(2 * K, 2 * WIDE).astype(ml_dtypes.bfloat16)


def row_tables():
    freq = np.arange(K) - K // 2
    place = np.arange(ROWS)
    group, lane = place // 8, place % 8
    even = lane % 2 == 0
    first = np.where(even, 8 * group + lane // 2, 8 * group + 4 + lane // 2)
    second = np.where(even, 8 * group + 4 + lane // 2, 8 * group + lane // 2)
    out = []
    for order in (first, second):
        phase = np.mod(order[:, None] * freq[None, :], NPIX) * (2.0 * math.pi / NPIX)
        cos, sin = np.cos(phase), np.sin(phase)
        out.append(np.block([[cos, -sin], [sin, cos]]))
    return np.stack(out).astype(ml_dtypes.bfloat16)


def interpolation_table():
    theta = 2.0 * math.pi * (np.arange(NPIX)[None, :] / NPIX - np.arange(SAMPLES)[:, None] / SAMPLES)
    half = np.sin(theta / 2)
    safe = np.where(np.abs(half) < 1e-12, 1.0, half)
    kernel = np.where(np.abs(half) < 1e-12, 1.0, np.sin(SAMPLES * theta / 2) / (SAMPLES * safe))
    table = np.zeros((WIDE, NPIX))
    table[:SAMPLES] = kernel
    high = table.astype(ml_dtypes.bfloat16)
    low = (table - high.astype(np.float64)).astype(ml_dtypes.bfloat16)
    return high, low


def layout_kernel(pupils, spectra, out, done):
    copies = []
    for piece in range(12):
        source = pupils.at[piece // 2, piece % 2] if piece < 8 else spectra.at[(piece - 8) // 2, piece % 2]
        copies.append(pltpu.make_async_copy(source, out.at[:, piece], done.at[piece]))
    for copy in copies:
        copy.start()
    for copy in copies:
        copy.wait()


def product_kernel(assignment, zone_of, density, held, out):
    slots = assignment.shape[0]
    per_device = slots // out.shape[0]
    sources = 4
    freq = lax.broadcasted_iota(jnp.int32, (8, K), 0) + lax.axis_index("tile") * 8 - K // 2
    distance = jnp.abs(freq) * 8
    for slot in range(slots):
        tile = assignment[slot]
        zone = zone_of[tile]
        keep = (distance < density[tile] * K).astype(jnp.float32)
        pupil = held[zone, 0:64, :].astype(jnp.float32).reshape(sources, 2, 8, K)
        start = pl.multiple_of(64 + 16 * (tile % 2), 16)
        mask = held[tile // 2, pl.ds(start, 16), :].astype(jnp.float32).reshape(2, 8, K) * keep
        real = pupil[:, 0] * mask[0] - pupil[:, 1] * mask[1]
        imag = pupil[:, 0] * mask[1] + pupil[:, 1] * mask[0]
        both = jnp.stack([real.reshape(2, 16, K), imag.reshape(2, 16, K)], 1).reshape(64, K)
        first = 64 * (slot % per_device)
        out[slot // per_device, first : first + 64, :] = both.astype(jnp.bfloat16)


def image_kernel(weights, products, columns, rows, out):
    stacked = []
    for piece in range(4):
        real = products[:, 32 * piece : 32 * piece + 16, :].reshape(2 * K, K)
        imag = products[:, 32 * piece + 16 : 32 * piece + 32, :].reshape(2 * K, K)
        stacked.append(jnp.concatenate([real, imag], 1))
    halves = jnp.dot(jnp.concatenate(stacked, 0), columns[...], preferred_element_type=jnp.float32)
    halves = halves.reshape(2, 2, K // 8, 2, 8, 2 * WIDE)
    images = []
    for slot in range(2):
        sides = []
        for source in range(4):
            half = halves[slot, source // 2, :, source % 2].reshape(K, 2 * WIDE).astype(jnp.bfloat16)
            sides.append(jnp.concatenate([half[:, :WIDE], half[:, WIDE:]], 0))
        field = jnp.dot(rows[slot], jnp.concatenate(sides, 1), preferred_element_type=jnp.float32)
        power = field[:ROWS] * field[:ROWS] + field[ROWS:] * field[ROWS:]
        total = jnp.zeros((ROWS, WIDE), jnp.float32)
        for source in range(4):
            total = total + weights[source].astype(jnp.float32) * power[:, source * WIDE : (source + 1) * WIDE]
        images.append(total)
    weight_sum = weights[0] + weights[1] + weights[2] + weights[3]
    last = lax.broadcasted_iota(jnp.int32, (ROWS, WIDE), 1) == SAMPLES
    even = lax.broadcasted_iota(jnp.int32, (ROWS, WIDE), 0) % 2 == 0
    first = jnp.where(last, weight_sum.astype(jnp.float32), images[0])
    second = jnp.where(last, weight_sum.astype(jnp.float32), images[1])
    lower = jnp.where(even, first, second).reshape(ROWS // 8, 8, WIDE)
    upper = jnp.where(even, pltpu.roll(first, ROWS - 1, 0), pltpu.roll(second, 1, 0)).reshape(ROWS // 8, 8, WIDE)
    out[...] = jnp.stack([lower, upper], 1).reshape(ROWS // 4, 8, WIDE).astype(out.dtype)


def finish_kernel(parts, high, low, out, held, done):
    summed = jnp.sum(parts[...].astype(jnp.float32), 0)
    total = summed[:, SAMPLES:]
    coarse = summed.astype(jnp.bfloat16)
    fine = (summed - coarse.astype(jnp.float32)).astype(jnp.bfloat16)
    both = jnp.concatenate([coarse, fine], 0)
    copies = []
    width = NPIX // 4
    for piece in range(4):
        cut = pl.ds(width * piece, width)
        by_high = jnp.dot(both, high[:, cut], preferred_element_type=jnp.float32)
        by_low = jnp.dot(coarse, low[:, cut], preferred_element_type=jnp.float32)
        result = (by_high[:8] + by_high[8:] + by_low) / total
        for row in range(4):
            held[row, :, cut] = result[2 * row : 2 * row + 2]
        copy = pltpu.make_async_copy(held.at[:, :, cut], out.at[:, :, cut], done.at[piece])
        copy.start()
        copies.append(copy)
    for copy in copies:
        copy.wait()


def shards(spectra, pupils, zone_of, density, assignment, weights):
    devices = lax.axis_size("tile")
    sources = pupils.shape[1]
    scalars = pl.BlockSpec(memory_space=pltpu.SMEM)
    blocks = pl.BlockSpec(memory_space=pltpu.VMEM)
    params = pltpu.CompilerParams(vmem_limit_bytes=VMEM_LIMIT)

    hbm = pl.BlockSpec(memory_space=pltpu.HBM)
    laid = pl.pallas_call(
        layout_kernel,
        out_shape=jax.ShapeDtypeStruct((devices, 12, 8, K), jnp.bfloat16),
        in_specs=[hbm, hbm],
        out_specs=blocks,
        scratch_shapes=[pltpu.SemaphoreType.DMA((12,))],
        compiler_params=params,
        name="layout",
    )(
        pltpu.with_memory_space_constraint(pupils.reshape(sources, 2, devices, 8, K), pltpu.HBM),
        pltpu.with_memory_space_constraint(spectra.reshape(2, 2, devices, 8, K), pltpu.HBM),
    )
    held = lax.all_to_all(laid.reshape(devices, 96, K), "tile", 0, 0, tiled=True)

    products = pl.pallas_call(
        product_kernel,
        out_shape=jax.ShapeDtypeStruct((devices, 2 * sources * 16, K), jnp.bfloat16),
        in_specs=[scalars] * 3 + [blocks],
        out_specs=blocks,
        compiler_params=params,
        name="products",
    )(assignment, zone_of, density, held)
    products = lax.all_to_all(products, "tile", 0, 0, tiled=True)

    image = pl.pallas_call(
        image_kernel,
        out_shape=jax.ShapeDtypeStruct((ROWS // 4, 8, WIDE), jnp.bfloat16),
        in_specs=[scalars] + [blocks] * 3,
        out_specs=blocks,
        compiler_params=params,
        name="images",
    )(weights, products, jnp.asarray(sample_table()), jnp.asarray(row_tables()))
    parts = lax.all_to_all(image, "src", 0, 0, tiled=True)

    high, low = interpolation_table()
    return pl.pallas_call(
        finish_kernel,
        out_shape=jax.ShapeDtypeStruct((4, 2, NPIX), jnp.float32),
        in_specs=[blocks] * 3,
        out_specs=hbm,
        scratch_shapes=[pltpu.VMEM((4, 2, NPIX), jnp.float32), pltpu.SemaphoreType.DMA((4,))],
        compiler_params=params,
        name="finish",
    )(parts, jnp.asarray(high), jnp.asarray(low))


def solution(mesh):
    return jax.shard_map(
        shards,
        mesh=mesh,
        in_specs=(
            P("tile", None, None, None),
            P("tile", "src", None, None, None),
            P(),
            P(),
            P(),
            P("src"),
        ),
        out_specs=P("src", "tile", None),
        check_vma=False,
    )
```

```python
import math

import jax
import jax.numpy as jnp
import ml_dtypes
import numpy as np
from jax import lax
from jax.experimental import pallas as pl
from jax.experimental.pallas import tpu as pltpu
from jax.sharding import PartitionSpec as P

K = 128
NPIX = 2048
ROWS = 128
SAMPLES = 255
WIDE = 256
VMEM_LIMIT = 48 * 1024 * 1024


def sample_table():
    freq = np.arange(K) - K // 2
    point = np.arange(SAMPLES)
    angle = np.mod(freq[:, None] * point[None, :], SAMPLES) * (2.0 * math.pi / SAMPLES)
    table = np.zeros((2, K, 2, WIDE))
    table[0, :, 0, :SAMPLES] = np.cos(angle)
    table[0, :, 1, :SAMPLES] = np.sin(angle)
    table[1, :, 0, :SAMPLES] = -np.sin(angle)
    table[1, :, 1, :SAMPLES] = np.cos(angle)
    return table.reshape(2 * K, 2 * WIDE).astype(ml_dtypes.bfloat16)


def row_tables():
    freq = np.arange(K) - K // 2
    place = np.arange(ROWS)
    group, lane = place // 8, place % 8
    even = lane % 2 == 0
    first = np.where(even, 8 * group + lane // 2, 8 * group + 4 + lane // 2)
    second = np.where(even, 8 * group + 4 + lane // 2, 8 * group + lane // 2)
    out = []
    for order in (first, second):
        phase = np.mod(order[:, None] * freq[None, :], NPIX) * (2.0 * math.pi / NPIX)
        cos, sin = np.cos(phase), np.sin(phase)
        out.append(np.block([[cos, -sin], [sin, cos]]))
    return np.stack(out).astype(ml_dtypes.bfloat16)


def interpolation_table():
    theta = 2.0 * math.pi * (np.arange(NPIX)[None, :] / NPIX - np.arange(SAMPLES)[:, None] / SAMPLES)
    half = np.sin(theta / 2)
    safe = np.where(np.abs(half) < 1e-12, 1.0, half)
    kernel = np.where(np.abs(half) < 1e-12, 1.0, np.sin(SAMPLES * theta / 2) / (SAMPLES * safe))
    table = np.zeros((WIDE, NPIX))
    table[:SAMPLES] = kernel
    high = table.astype(ml_dtypes.bfloat16)
    low = (table - high.astype(np.float64)).astype(ml_dtypes.bfloat16)
    return high, low


def layout_kernel(pupils, spectra, assignment, zone_of, density, weights, out, tiles, zones, levels, shares, done):
    copies = [
        pltpu.make_async_copy(assignment, tiles, done.at[12]),
        pltpu.make_async_copy(zone_of, zones, done.at[13]),
        pltpu.make_async_copy(density, levels, done.at[14]),
        pltpu.make_async_copy(weights, shares, done.at[15]),
    ]
    for piece in range(12):
        source = pupils.at[piece // 2, piece % 2] if piece < 8 else spectra.at[(piece - 8) // 2, piece % 2]
        copies.append(pltpu.make_async_copy(source, out.at[:, piece], done.at[piece]))
    for copy in copies:
        copy.start()
    for copy in copies:
        copy.wait()


def product_kernel(assignment, zone_of, density, held, out):
    slots = assignment.shape[0]
    per_device = slots // out.shape[0]
    sources = 4
    freq = lax.broadcasted_iota(jnp.int32, (8, K), 0) + lax.axis_index("tile") * 8 - K // 2
    distance = jnp.abs(freq) * 8
    for slot in range(slots):
        tile = assignment[slot]
        zone = zone_of[tile]
        keep = (distance < density[tile] * K).astype(jnp.float32)
        pupil = held[zone, 0:64, :].astype(jnp.float32).reshape(sources, 2, 8, K)
        start = pl.multiple_of(64 + 16 * (tile % 2), 16)
        mask = held[tile // 2, pl.ds(start, 16), :].astype(jnp.float32).reshape(2, 8, K) * keep
        real = pupil[:, 0] * mask[0] - pupil[:, 1] * mask[1]
        imag = pupil[:, 0] * mask[1] + pupil[:, 1] * mask[0]
        both = jnp.stack([real.reshape(2, 16, K), imag.reshape(2, 16, K)], 1).reshape(64, K)
        first = 64 * (slot % per_device)
        out[slot // per_device, first : first + 64, :] = both.astype(jnp.bfloat16)


def image_kernel(weights, products, columns, rows, out):
    stacked = []
    for piece in range(4):
        real = products[:, 32 * piece : 32 * piece + 16, :].reshape(2 * K, K)
        imag = products[:, 32 * piece + 16 : 32 * piece + 32, :].reshape(2 * K, K)
        stacked.append(jnp.concatenate([real, imag], 1))
    halves = jnp.dot(jnp.concatenate(stacked, 0), columns[...], preferred_element_type=jnp.float32)
    halves = halves.reshape(2, 2, K // 8, 2, 8, 2 * WIDE)
    images = []
    for slot in range(2):
        sides = []
        for source in range(4):
            half = halves[slot, source // 2, :, source % 2].reshape(K, 2 * WIDE).astype(jnp.bfloat16)
            sides.append(jnp.concatenate([half[:, :WIDE], half[:, WIDE:]], 0))
        field = jnp.dot(rows[slot], jnp.concatenate(sides, 1), preferred_element_type=jnp.float32)
        power = field[:ROWS] * field[:ROWS] + field[ROWS:] * field[ROWS:]
        total = jnp.zeros((ROWS, WIDE), jnp.float32)
        for source in range(4):
            total = total + weights[source].astype(jnp.float32) * power[:, source * WIDE : (source + 1) * WIDE]
        images.append(total)
    weight_sum = weights[0] + weights[1] + weights[2] + weights[3]
    last = lax.broadcasted_iota(jnp.int32, (ROWS, WIDE), 1) == SAMPLES
    even = lax.broadcasted_iota(jnp.int32, (ROWS, WIDE), 0) % 2 == 0
    first = jnp.where(last, weight_sum.astype(jnp.float32), images[0])
    second = jnp.where(last, weight_sum.astype(jnp.float32), images[1])
    lower = jnp.where(even, first, second).reshape(ROWS // 8, 8, WIDE)
    upper = jnp.where(even, pltpu.roll(first, ROWS - 1, 0), pltpu.roll(second, 1, 0)).reshape(ROWS // 8, 8, WIDE)
    out[...] = jnp.stack([lower, upper], 1).reshape(ROWS // 4, 8, WIDE).astype(out.dtype)


def finish_kernel(parts, high, low, out, held, done):
    summed = jnp.sum(parts[...].astype(jnp.float32), 0)
    total = summed[:, SAMPLES:]
    coarse = summed.astype(jnp.bfloat16)
    fine = (summed - coarse.astype(jnp.float32)).astype(jnp.bfloat16)
    both = jnp.concatenate([coarse, fine], 0)
    copies = []
    width = NPIX // 4
    for piece in range(4):
        cut = pl.ds(width * piece, width)
        by_high = jnp.dot(both, high[:, cut], preferred_element_type=jnp.float32)
        by_low = jnp.dot(coarse, low[:, cut], preferred_element_type=jnp.float32)
        result = (by_high[:8] + by_high[8:] + by_low) / total
        for row in range(4):
            held[row, :, cut] = result[2 * row : 2 * row + 2]
        copy = pltpu.make_async_copy(held.at[:, :, cut], out.at[:, :, cut], done.at[piece])
        copy.start()
        copies.append(copy)
    for copy in copies:
        copy.wait()


def shards(spectra, pupils, zone_of, density, assignment, weights):
    devices = lax.axis_size("tile")
    sources = pupils.shape[1]
    scalars = pl.BlockSpec(memory_space=pltpu.SMEM)
    blocks = pl.BlockSpec(memory_space=pltpu.VMEM)
    params = pltpu.CompilerParams(vmem_limit_bytes=VMEM_LIMIT)

    hbm = pl.BlockSpec(memory_space=pltpu.HBM)
    tables = [assignment, zone_of, density, weights]
    laid, assignment, zone_of, density, weights = pl.pallas_call(
        layout_kernel,
        out_shape=[jax.ShapeDtypeStruct((devices, 12, 8, K), jnp.bfloat16)] + [pltpu.SMEM(x.shape, x.dtype) for x in tables],
        in_specs=[hbm] * 6,
        out_specs=[blocks] + [scalars] * 4,
        scratch_shapes=[pltpu.SemaphoreType.DMA((16,))],
        compiler_params=params,
        name="layout",
    )(
        pltpu.with_memory_space_constraint(pupils.reshape(sources, 2, devices, 8, K), pltpu.HBM),
        pltpu.with_memory_space_constraint(spectra.reshape(2, 2, devices, 8, K), pltpu.HBM),
        *(pltpu.with_memory_space_constraint(x, pltpu.HBM) for x in tables),
    )
    held = lax.all_to_all(laid.reshape(devices, 96, K), "tile", 0, 0, tiled=True)

    products = pl.pallas_call(
        product_kernel,
        out_shape=jax.ShapeDtypeStruct((devices, 2 * sources * 16, K), jnp.bfloat16),
        in_specs=[scalars] * 3 + [blocks],
        out_specs=blocks,
        compiler_params=params,
        name="products",
    )(assignment, zone_of, density, held)
    products = lax.all_to_all(products, "tile", 0, 0, tiled=True)

    image = pl.pallas_call(
        image_kernel,
        out_shape=jax.ShapeDtypeStruct((ROWS // 4, 8, WIDE), jnp.bfloat16),
        in_specs=[scalars] + [blocks] * 3,
        out_specs=blocks,
        compiler_params=params,
        name="images",
    )(weights, products, jnp.asarray(sample_table()), jnp.asarray(row_tables()))
    parts = lax.all_to_all(image, "src", 0, 0, tiled=True)

    high, low = interpolation_table()
    return pl.pallas_call(
        finish_kernel,
        out_shape=jax.ShapeDtypeStruct((4, 2, NPIX), jnp.float32),
        in_specs=[blocks] * 3,
        out_specs=hbm,
        scratch_shapes=[pltpu.VMEM((4, 2, NPIX), jnp.float32), pltpu.SemaphoreType.DMA((4,))],
        compiler_params=params,
        name="finish",
    )(parts, jnp.asarray(high), jnp.asarray(low))


def solution(mesh):
    return jax.shard_map(
        shards,
        mesh=mesh,
        in_specs=(
            P("tile", None, None, None),
            P("tile", "src", None, None, None),
            P(),
            P(),
            P(),
            P("src"),
        ),
        out_specs=P("src", "tile", None),
        check_vma=False,
    )
```

```python
import math

import jax
import jax.numpy as jnp
import ml_dtypes
import numpy as np
from jax import lax
from jax.experimental import pallas as pl
from jax.experimental.pallas import tpu as pltpu
from jax.sharding import PartitionSpec as P

K = 128
NPIX = 2048
ROWS = 128
SAMPLES = 255
WIDE = 256
VMEM_LIMIT = 48 * 1024 * 1024


def sample_table():
    freq = np.arange(K) - K // 2
    point = np.arange(SAMPLES)
    angle = np.mod(freq[:, None] * point[None, :], SAMPLES) * (2.0 * math.pi / SAMPLES)
    table = np.zeros((2, K, 2, WIDE))
    table[0, :, 0, :SAMPLES] = np.cos(angle)
    table[0, :, 1, :SAMPLES] = np.sin(angle)
    table[1, :, 0, :SAMPLES] = -np.sin(angle)
    table[1, :, 1, :SAMPLES] = np.cos(angle)
    table = table.reshape(2 * K, 2 * WIDE)
    high = table.astype(ml_dtypes.bfloat16)
    return np.stack([high, (table - high.astype(np.float64)).astype(ml_dtypes.bfloat16)])


def row_tables():
    freq = np.arange(K) - K // 2
    place = np.arange(ROWS)
    group, lane = place // 8, place % 8
    even = lane % 2 == 0
    first = np.where(even, 8 * group + lane // 2, 8 * group + 4 + lane // 2)
    second = np.where(even, 8 * group + 4 + lane // 2, 8 * group + lane // 2)
    out = []
    for order in (first, second):
        phase = np.mod(order[:, None] * freq[None, :], NPIX) * (2.0 * math.pi / NPIX)
        cos, sin = np.cos(phase), np.sin(phase)
        out.append(np.block([[cos, -sin], [sin, cos]]))
    return np.stack(out).astype(ml_dtypes.bfloat16)


def interpolation_table():
    theta = 2.0 * math.pi * (np.arange(NPIX)[None, :] / NPIX - np.arange(SAMPLES)[:, None] / SAMPLES)
    half = np.sin(theta / 2)
    safe = np.where(np.abs(half) < 1e-12, 1.0, half)
    kernel = np.where(np.abs(half) < 1e-12, 1.0, np.sin(SAMPLES * theta / 2) / (SAMPLES * safe))
    table = np.zeros((WIDE, NPIX))
    table[:SAMPLES] = kernel
    high = table.astype(ml_dtypes.bfloat16)
    low = (table - high.astype(np.float64)).astype(ml_dtypes.bfloat16)
    return high, low


def layout_kernel(pupils, spectra, assignment, zone_of, density, weights, out, tiles, zones, levels, shares, done):
    copies = [
        pltpu.make_async_copy(assignment, tiles, done.at[12]),
        pltpu.make_async_copy(zone_of, zones, done.at[13]),
        pltpu.make_async_copy(density, levels, done.at[14]),
        pltpu.make_async_copy(weights, shares, done.at[15]),
    ]
    for piece in range(12):
        source = pupils.at[piece // 2, piece % 2] if piece < 8 else spectra.at[(piece - 8) // 2, piece % 2]
        copies.append(pltpu.make_async_copy(source, out.at[:, piece], done.at[piece]))
    for copy in copies:
        copy.start()
    for copy in copies:
        copy.wait()


def product_kernel(assignment, zone_of, density, held, out):
    slots = assignment.shape[0]
    per_device = slots // out.shape[0]
    sources = 4
    freq = lax.broadcasted_iota(jnp.int32, (8, K), 0) + lax.axis_index("tile") * 8 - K // 2
    distance = jnp.abs(freq) * 8
    for slot in range(slots):
        tile = assignment[slot]
        zone = zone_of[tile]
        keep = (distance < density[tile] * K).astype(jnp.float32)
        pupil = held[zone, 0:64, :].astype(jnp.float32).reshape(sources, 2, 8, K)
        start = pl.multiple_of(64 + 16 * (tile % 2), 16)
        mask = held[tile // 2, pl.ds(start, 16), :].astype(jnp.float32).reshape(2, 8, K) * keep
        real = pupil[:, 0] * mask[0] - pupil[:, 1] * mask[1]
        imag = pupil[:, 0] * mask[1] + pupil[:, 1] * mask[0]
        both = jnp.stack([real.reshape(2, 16, K), imag.reshape(2, 16, K)], 1).reshape(64, K)
        first = 64 * (slot % per_device)
        out[slot // per_device, first : first + 64, :] = both.astype(jnp.bfloat16)


def image_kernel(weights, products, columns, rows, out):
    stacked = []
    for piece in range(4):
        real = products[:, 32 * piece : 32 * piece + 16, :].reshape(2 * K, K)
        imag = products[:, 32 * piece + 16 : 32 * piece + 32, :].reshape(2 * K, K)
        stacked.append(jnp.concatenate([real, imag], 1))
    stacked = jnp.concatenate(stacked, 0)
    halves = jnp.dot(stacked, columns[0], preferred_element_type=jnp.float32)
    halves = halves + jnp.dot(stacked, columns[1], preferred_element_type=jnp.float32)
    halves = halves.reshape(2, 2, K // 8, 2, 8, 2 * WIDE)
    images = []
    for slot in range(2):
        sides = []
        for source in range(4):
            half = halves[slot, source // 2, :, source % 2].reshape(K, 2 * WIDE).astype(jnp.bfloat16)
            sides.append(jnp.concatenate([half[:, :WIDE], half[:, WIDE:]], 0))
        field = jnp.dot(rows[slot], jnp.concatenate(sides, 1), preferred_element_type=jnp.float32)
        power = field[:ROWS] * field[:ROWS] + field[ROWS:] * field[ROWS:]
        total = jnp.zeros((ROWS, WIDE), jnp.float32)
        for source in range(4):
            total = total + weights[source].astype(jnp.float32) * power[:, source * WIDE : (source + 1) * WIDE]
        images.append(total)
    weight_sum = weights[0] + weights[1] + weights[2] + weights[3]
    last = lax.broadcasted_iota(jnp.int32, (ROWS, WIDE), 1) == SAMPLES
    even = lax.broadcasted_iota(jnp.int32, (ROWS, WIDE), 0) % 2 == 0
    first = jnp.where(last, weight_sum.astype(jnp.float32), images[0])
    second = jnp.where(last, weight_sum.astype(jnp.float32), images[1])
    lower = jnp.where(even, first, second).reshape(ROWS // 8, 8, WIDE)
    upper = jnp.where(even, pltpu.roll(first, ROWS - 1, 0), pltpu.roll(second, 1, 0)).reshape(ROWS // 8, 8, WIDE)
    out[...] = jnp.stack([lower, upper], 1).reshape(ROWS // 4, 8, WIDE).astype(out.dtype)


def finish_kernel(parts, high, low, out, held, done):
    summed = jnp.sum(parts[...].astype(jnp.float32), 0)
    total = summed[:, SAMPLES:]
    coarse = summed.astype(jnp.bfloat16)
    fine = (summed - coarse.astype(jnp.float32)).astype(jnp.bfloat16)
    both = jnp.concatenate([coarse, fine], 0)
    copies = []
    width = NPIX // 4
    for piece in range(4):
        cut = pl.ds(width * piece, width)
        by_high = jnp.dot(both, high[:, cut], preferred_element_type=jnp.float32)
        by_low = jnp.dot(coarse, low[:, cut], preferred_element_type=jnp.float32)
        result = (by_high[:8] + by_high[8:] + by_low) / total
        for row in range(4):
            held[row, :, cut] = result[2 * row : 2 * row + 2]
        copy = pltpu.make_async_copy(held.at[:, :, cut], out.at[:, :, cut], done.at[piece])
        copy.start()
        copies.append(copy)
    for copy in copies:
        copy.wait()


def shards(spectra, pupils, zone_of, density, assignment, weights):
    devices = lax.axis_size("tile")
    sources = pupils.shape[1]
    scalars = pl.BlockSpec(memory_space=pltpu.SMEM)
    blocks = pl.BlockSpec(memory_space=pltpu.VMEM)
    params = pltpu.CompilerParams(vmem_limit_bytes=VMEM_LIMIT)

    hbm = pl.BlockSpec(memory_space=pltpu.HBM)
    tables = [assignment, zone_of, density, weights]
    laid, assignment, zone_of, density, weights = pl.pallas_call(
        layout_kernel,
        out_shape=[jax.ShapeDtypeStruct((devices, 12, 8, K), jnp.bfloat16)] + [pltpu.SMEM(x.shape, x.dtype) for x in tables],
        in_specs=[hbm] * 6,
        out_specs=[blocks] + [scalars] * 4,
        scratch_shapes=[pltpu.SemaphoreType.DMA((16,))],
        compiler_params=params,
        name="layout",
    )(
        pltpu.with_memory_space_constraint(pupils.reshape(sources, 2, devices, 8, K), pltpu.HBM),
        pltpu.with_memory_space_constraint(spectra.reshape(2, 2, devices, 8, K), pltpu.HBM),
        *(pltpu.with_memory_space_constraint(x, pltpu.HBM) for x in tables),
    )
    held = lax.all_to_all(laid.reshape(devices, 96, K), "tile", 0, 0, tiled=True)

    products = pl.pallas_call(
        product_kernel,
        out_shape=jax.ShapeDtypeStruct((devices, 2 * sources * 16, K), jnp.bfloat16),
        in_specs=[scalars] * 3 + [blocks],
        out_specs=blocks,
        compiler_params=params,
        name="products",
    )(assignment, zone_of, density, held)
    products = lax.all_to_all(products, "tile", 0, 0, tiled=True)

    image = pl.pallas_call(
        image_kernel,
        out_shape=jax.ShapeDtypeStruct((ROWS // 4, 8, WIDE), jnp.bfloat16),
        in_specs=[scalars] + [blocks] * 3,
        out_specs=blocks,
        compiler_params=params,
        name="images",
    )(weights, products, jnp.asarray(sample_table()), jnp.asarray(row_tables()))
    parts = lax.all_to_all(image, "src", 0, 0, tiled=True)

    high, low = interpolation_table()
    return pl.pallas_call(
        finish_kernel,
        out_shape=jax.ShapeDtypeStruct((4, 2, NPIX), jnp.float32),
        in_specs=[blocks] * 3,
        out_specs=hbm,
        scratch_shapes=[pltpu.VMEM((4, 2, NPIX), jnp.float32), pltpu.SemaphoreType.DMA((4,))],
        compiler_params=params,
        name="finish",
    )(parts, jnp.asarray(high), jnp.asarray(low))


def solution(mesh):
    return jax.shard_map(
        shards,
        mesh=mesh,
        in_specs=(
            P("tile", None, None, None),
            P("tile", "src", None, None, None),
            P(),
            P(),
            P(),
            P("src"),
        ),
        out_specs=P("src", "tile", None),
        check_vma=False,
    )
```

```python
import math

import jax
import jax.numpy as jnp
import ml_dtypes
import numpy as np
from jax import lax
from jax.experimental import pallas as pl
from jax.experimental.pallas import tpu as pltpu
from jax.sharding import PartitionSpec as P

K = 128
NPIX = 2048
ROWS = 128
SAMPLES = 255
OFFSET = 0.24825
WIDE = 256
VMEM_LIMIT = 48 * 1024 * 1024


def sample_table():
    freq = np.arange(K) - K // 2
    point = np.arange(SAMPLES) + OFFSET
    angle = freq[:, None] * point[None, :] * (2.0 * math.pi / SAMPLES)
    table = np.zeros((2, K, 2, WIDE))
    table[0, :, 0, :SAMPLES] = np.cos(angle)
    table[0, :, 1, :SAMPLES] = np.sin(angle)
    table[1, :, 0, :SAMPLES] = -np.sin(angle)
    table[1, :, 1, :SAMPLES] = np.cos(angle)
    return table.reshape(2 * K, 2 * WIDE).astype(ml_dtypes.bfloat16)


def row_tables():
    freq = np.arange(K) - K // 2
    place = np.arange(ROWS)
    group, lane = place // 8, place % 8
    even = lane % 2 == 0
    first = np.where(even, 8 * group + lane // 2, 8 * group + 4 + lane // 2)
    second = np.where(even, 8 * group + 4 + lane // 2, 8 * group + lane // 2)
    out = []
    for order in (first, second):
        phase = np.mod(order[:, None] * freq[None, :], NPIX) * (2.0 * math.pi / NPIX)
        cos, sin = np.cos(phase), np.sin(phase)
        out.append(np.block([[cos, -sin], [sin, cos]]))
    return np.stack(out).astype(ml_dtypes.bfloat16)


def interpolation_table():
    theta = 2.0 * math.pi * (np.arange(NPIX)[None, :] / NPIX - (np.arange(SAMPLES)[:, None] + OFFSET) / SAMPLES)
    half = np.sin(theta / 2)
    safe = np.where(np.abs(half) < 1e-12, 1.0, half)
    kernel = np.where(np.abs(half) < 1e-12, 1.0, np.sin(SAMPLES * theta / 2) / (SAMPLES * safe))
    table = np.zeros((WIDE, NPIX))
    table[:SAMPLES] = kernel
    high = table.astype(ml_dtypes.bfloat16)
    low = (table - high.astype(np.float64)).astype(ml_dtypes.bfloat16)
    return high, low


def layout_kernel(pupils, spectra, assignment, zone_of, density, weights, out, tiles, zones, levels, shares, done):
    copies = [
        pltpu.make_async_copy(assignment, tiles, done.at[12]),
        pltpu.make_async_copy(zone_of, zones, done.at[13]),
        pltpu.make_async_copy(density, levels, done.at[14]),
        pltpu.make_async_copy(weights, shares, done.at[15]),
    ]
    for piece in range(12):
        source = pupils.at[piece // 2, piece % 2] if piece < 8 else spectra.at[(piece - 8) // 2, piece % 2]
        copies.append(pltpu.make_async_copy(source, out.at[:, piece], done.at[piece]))
    for copy in copies:
        copy.start()
    for copy in copies:
        copy.wait()


def product_kernel(assignment, zone_of, density, held, out):
    slots = assignment.shape[0]
    per_device = slots // out.shape[0]
    sources = 4
    freq = lax.broadcasted_iota(jnp.int32, (8, K), 0) + lax.axis_index("tile") * 8 - K // 2
    distance = jnp.abs(freq) * 8
    for slot in range(slots):
        tile = assignment[slot]
        zone = zone_of[tile]
        keep = (distance < density[tile] * K).astype(jnp.float32)
        pupil = held[zone, 0:64, :].astype(jnp.float32).reshape(sources, 2, 8, K)
        start = pl.multiple_of(64 + 16 * (tile % 2), 16)
        mask = held[tile // 2, pl.ds(start, 16), :].astype(jnp.float32).reshape(2, 8, K) * keep
        real = pupil[:, 0] * mask[0] - pupil[:, 1] * mask[1]
        imag = pupil[:, 0] * mask[1] + pupil[:, 1] * mask[0]
        both = jnp.stack([real.reshape(2, 16, K), imag.reshape(2, 16, K)], 1).reshape(64, K)
        first = 64 * (slot % per_device)
        out[slot // per_device, first : first + 64, :] = both.astype(jnp.bfloat16)


def image_kernel(weights, products, columns, rows, out):
    stacked = []
    for piece in range(4):
        real = products[:, 32 * piece : 32 * piece + 16, :].reshape(2 * K, K)
        imag = products[:, 32 * piece + 16 : 32 * piece + 32, :].reshape(2 * K, K)
        stacked.append(jnp.concatenate([real, imag], 1))
    halves = jnp.dot(jnp.concatenate(stacked, 0), columns[...], preferred_element_type=jnp.float32)
    halves = halves.reshape(2, 2, K // 8, 2, 8, 2 * WIDE)
    images = []
    for slot in range(2):
        sides = []
        for source in range(4):
            half = halves[slot, source // 2, :, source % 2].reshape(K, 2 * WIDE).astype(jnp.bfloat16)
            sides.append(jnp.concatenate([half[:, :WIDE], half[:, WIDE:]], 0))
        field = jnp.dot(rows[slot], jnp.concatenate(sides, 1), preferred_element_type=jnp.float32)
        power = field[:ROWS] * field[:ROWS] + field[ROWS:] * field[ROWS:]
        total = jnp.zeros((ROWS, WIDE), jnp.float32)
        for source in range(4):
            total = total + weights[source].astype(jnp.float32) * power[:, source * WIDE : (source + 1) * WIDE]
        images.append(total)
    weight_sum = weights[0] + weights[1] + weights[2] + weights[3]
    last = lax.broadcasted_iota(jnp.int32, (ROWS, WIDE), 1) == SAMPLES
    even = lax.broadcasted_iota(jnp.int32, (ROWS, WIDE), 0) % 2 == 0
    first = jnp.where(last, weight_sum.astype(jnp.float32), images[0])
    second = jnp.where(last, weight_sum.astype(jnp.float32), images[1])
    lower = jnp.where(even, first, second).reshape(ROWS // 8, 8, WIDE)
    upper = jnp.where(even, pltpu.roll(first, ROWS - 1, 0), pltpu.roll(second, 1, 0)).reshape(ROWS // 8, 8, WIDE)
    out[...] = jnp.stack([lower, upper], 1).reshape(ROWS // 4, 8, WIDE).astype(out.dtype)


def finish_kernel(parts, high, low, out, held, done):
    summed = jnp.sum(parts[...].astype(jnp.float32), 0)
    total = summed[:, SAMPLES:]
    coarse = summed.astype(jnp.bfloat16)
    fine = (summed - coarse.astype(jnp.float32)).astype(jnp.bfloat16)
    both = jnp.concatenate([coarse, fine], 0)
    copies = []
    width = NPIX // 4
    for piece in range(4):
        cut = pl.ds(width * piece, width)
        by_high = jnp.dot(both, high[:, cut], preferred_element_type=jnp.float32)
        by_low = jnp.dot(coarse, low[:, cut], preferred_element_type=jnp.float32)
        result = (by_high[:8] + by_high[8:] + by_low) / total
        for row in range(4):
            held[row, :, cut] = result[2 * row : 2 * row + 2]
        copy = pltpu.make_async_copy(held.at[:, :, cut], out.at[:, :, cut], done.at[piece])
        copy.start()
        copies.append(copy)
    for copy in copies:
        copy.wait()


def shards(spectra, pupils, zone_of, density, assignment, weights):
    devices = lax.axis_size("tile")
    sources = pupils.shape[1]
    scalars = pl.BlockSpec(memory_space=pltpu.SMEM)
    blocks = pl.BlockSpec(memory_space=pltpu.VMEM)
    params = pltpu.CompilerParams(vmem_limit_bytes=VMEM_LIMIT)

    hbm = pl.BlockSpec(memory_space=pltpu.HBM)
    tables = [assignment, zone_of, density, weights]
    laid, assignment, zone_of, density, weights = pl.pallas_call(
        layout_kernel,
        out_shape=[jax.ShapeDtypeStruct((devices, 12, 8, K), jnp.bfloat16)] + [pltpu.SMEM(x.shape, x.dtype) for x in tables],
        in_specs=[hbm] * 6,
        out_specs=[blocks] + [scalars] * 4,
        scratch_shapes=[pltpu.SemaphoreType.DMA((16,))],
        compiler_params=params,
        name="layout",
    )(
        pltpu.with_memory_space_constraint(pupils.reshape(sources, 2, devices, 8, K), pltpu.HBM),
        pltpu.with_memory_space_constraint(spectra.reshape(2, 2, devices, 8, K), pltpu.HBM),
        *(pltpu.with_memory_space_constraint(x, pltpu.HBM) for x in tables),
    )
    held = lax.all_to_all(laid.reshape(devices, 96, K), "tile", 0, 0, tiled=True)

    products = pl.pallas_call(
        product_kernel,
        out_shape=jax.ShapeDtypeStruct((devices, 2 * sources * 16, K), jnp.bfloat16),
        in_specs=[scalars] * 3 + [blocks],
        out_specs=blocks,
        compiler_params=params,
        name="products",
    )(assignment, zone_of, density, held)
    products = lax.all_to_all(products, "tile", 0, 0, tiled=True)

    image = pl.pallas_call(
        image_kernel,
        out_shape=jax.ShapeDtypeStruct((ROWS // 4, 8, WIDE), jnp.bfloat16),
        in_specs=[scalars] + [blocks] * 3,
        out_specs=blocks,
        compiler_params=params,
        name="images",
    )(weights, products, jnp.asarray(sample_table()), jnp.asarray(row_tables()))
    parts = lax.all_to_all(image, "src", 0, 0, tiled=True)

    high, low = interpolation_table()
    return pl.pallas_call(
        finish_kernel,
        out_shape=jax.ShapeDtypeStruct((4, 2, NPIX), jnp.float32),
        in_specs=[blocks] * 3,
        out_specs=hbm,
        scratch_shapes=[pltpu.VMEM((4, 2, NPIX), jnp.float32), pltpu.SemaphoreType.DMA((4,))],
        compiler_params=params,
        name="finish",
    )(parts, jnp.asarray(high), jnp.asarray(low))


def solution(mesh):
    return jax.shard_map(
        shards,
        mesh=mesh,
        in_specs=(
            P("tile", None, None, None),
            P("tile", "src", None, None, None),
            P(),
            P(),
            P(),
            P("src"),
        ),
        out_specs=P("src", "tile", None),
        check_vma=False,
    )
```

```python
import math

import jax
import jax.numpy as jnp
import ml_dtypes
import numpy as np
from jax import lax
from jax.experimental import pallas as pl
from jax.experimental.pallas import tpu as pltpu
from jax.sharding import PartitionSpec as P

K = 128
NPIX = 2048
ROWS = 128
SAMPLES = 255
OFFSET = 0.24825
WIDE = 256
VMEM_LIMIT = 48 * 1024 * 1024


def sample_table():
    freq = np.arange(K) - K // 2
    point = np.arange(SAMPLES) + OFFSET
    angle = freq[:, None] * point[None, :] * (2.0 * math.pi / SAMPLES)
    table = np.zeros((2, K, 2, WIDE))
    table[0, :, 0, :SAMPLES] = np.cos(angle)
    table[0, :, 1, :SAMPLES] = np.sin(angle)
    table[1, :, 0, :SAMPLES] = -np.sin(angle)
    table[1, :, 1, :SAMPLES] = np.cos(angle)
    return table.reshape(2 * K, 2 * WIDE).astype(ml_dtypes.bfloat16)


def row_tables():
    freq = np.arange(K) - K // 2
    place = np.arange(ROWS)
    group, lane = place // 8, place % 8
    even = lane % 2 == 0
    first = np.where(even, 8 * group + lane // 2, 8 * group + 4 + lane // 2)
    second = np.where(even, 8 * group + 4 + lane // 2, 8 * group + lane // 2)
    out = []
    for order in (first, second):
        phase = np.mod(order[:, None] * freq[None, :], NPIX) * (2.0 * math.pi / NPIX)
        cos, sin = np.cos(phase), np.sin(phase)
        out.append(np.block([[cos, -sin], [sin, cos]]))
    return np.stack(out).astype(ml_dtypes.bfloat16)


def interpolation_table():
    theta = 2.0 * math.pi * (np.arange(NPIX)[None, :] / NPIX - (np.arange(SAMPLES)[:, None] + OFFSET) / SAMPLES)
    half = np.sin(theta / 2)
    safe = np.where(np.abs(half) < 1e-12, 1.0, half)
    kernel = np.where(np.abs(half) < 1e-12, 1.0, np.sin(SAMPLES * theta / 2) / (SAMPLES * safe))
    table = np.zeros((WIDE, NPIX))
    table[:SAMPLES] = kernel
    return table.astype(ml_dtypes.bfloat16)


def layout_kernel(pupils, spectra, assignment, zone_of, density, weights, out, tiles, zones, levels, shares, done):
    copies = [
        pltpu.make_async_copy(assignment, tiles, done.at[12]),
        pltpu.make_async_copy(zone_of, zones, done.at[13]),
        pltpu.make_async_copy(density, levels, done.at[14]),
        pltpu.make_async_copy(weights, shares, done.at[15]),
    ]
    for piece in range(12):
        source = pupils.at[piece // 2, piece % 2] if piece < 8 else spectra.at[(piece - 8) // 2, piece % 2]
        copies.append(pltpu.make_async_copy(source, out.at[:, piece], done.at[piece]))
    for copy in copies:
        copy.start()
    for copy in copies:
        copy.wait()


def product_kernel(assignment, zone_of, density, held, out):
    slots = assignment.shape[0]
    per_device = slots // out.shape[0]
    sources = 4
    freq = lax.broadcasted_iota(jnp.int32, (8, K), 0) + lax.axis_index("tile") * 8 - K // 2
    distance = jnp.abs(freq) * 8
    for slot in range(slots):
        tile = assignment[slot]
        zone = zone_of[tile]
        keep = (distance < density[tile] * K).astype(jnp.float32)
        pupil = held[zone, 0:64, :].astype(jnp.float32).reshape(sources, 2, 8, K)
        start = pl.multiple_of(64 + 16 * (tile % 2), 16)
        mask = held[tile // 2, pl.ds(start, 16), :].astype(jnp.float32).reshape(2, 8, K) * keep
        real = pupil[:, 0] * mask[0] - pupil[:, 1] * mask[1]
        imag = pupil[:, 0] * mask[1] + pupil[:, 1] * mask[0]
        both = jnp.stack([real.reshape(2, 16, K), imag.reshape(2, 16, K)], 1).reshape(64, K)
        first = 64 * (slot % per_device)
        out[slot // per_device, first : first + 64, :] = both.astype(jnp.bfloat16)


def image_kernel(weights, products, columns, rows, out):
    stacked = []
    for piece in range(4):
        real = products[:, 32 * piece : 32 * piece + 16, :].reshape(2 * K, K)
        imag = products[:, 32 * piece + 16 : 32 * piece + 32, :].reshape(2 * K, K)
        stacked.append(jnp.concatenate([real, imag], 1))
    halves = jnp.dot(jnp.concatenate(stacked, 0), columns[...], preferred_element_type=jnp.float32)
    halves = halves.reshape(2, 2, K // 8, 2, 8, 2 * WIDE)
    images = []
    for slot in range(2):
        sides = []
        for source in range(4):
            half = halves[slot, source // 2, :, source % 2].reshape(K, 2 * WIDE).astype(jnp.bfloat16)
            sides.append(jnp.concatenate([half[:, :WIDE], half[:, WIDE:]], 0))
        field = jnp.dot(rows[slot], jnp.concatenate(sides, 1), preferred_element_type=jnp.float32)
        power = field[:ROWS] * field[:ROWS] + field[ROWS:] * field[ROWS:]
        total = jnp.zeros((ROWS, WIDE), jnp.float32)
        for source in range(4):
            total = total + weights[source].astype(jnp.float32) * power[:, source * WIDE : (source + 1) * WIDE]
        images.append(total)
    weight_sum = weights[0] + weights[1] + weights[2] + weights[3]
    last = lax.broadcasted_iota(jnp.int32, (ROWS, WIDE), 1) == SAMPLES
    even = lax.broadcasted_iota(jnp.int32, (ROWS, WIDE), 0) % 2 == 0
    first = jnp.where(last, weight_sum.astype(jnp.float32), images[0])
    second = jnp.where(last, weight_sum.astype(jnp.float32), images[1])
    lower = jnp.where(even, first, second).reshape(ROWS // 8, 8, WIDE)
    upper = jnp.where(even, pltpu.roll(first, ROWS - 1, 0), pltpu.roll(second, 1, 0)).reshape(ROWS // 8, 8, WIDE)
    out[...] = jnp.stack([lower, upper], 1).reshape(ROWS // 4, 8, WIDE).astype(out.dtype)


def finish_kernel(parts, table, out, held, done):
    summed = jnp.sum(parts[...].astype(jnp.float32), 0)
    total = summed[:, SAMPLES:]
    inside = lax.broadcasted_iota(jnp.int32, summed.shape, 1) < SAMPLES
    mean = jnp.sum(jnp.where(inside, summed, 0.0), 1, keepdims=True) * (1.0 / SAMPLES)
    rest = jnp.where(inside, summed - mean, 0.0)
    coarse = rest.astype(jnp.bfloat16)
    fine = (rest - coarse.astype(jnp.float32)).astype(jnp.bfloat16)
    both = jnp.concatenate([coarse, fine], 0)
    copies = []
    width = NPIX // 2
    for piece in range(2):
        cut = pl.ds(width * piece, width)
        spread = jnp.dot(both, table[:, cut], preferred_element_type=jnp.float32)
        result = (mean + (spread[:8] + spread[8:])) / total
        for row in range(4):
            held[row, :, cut] = result[2 * row : 2 * row + 2]
        copy = pltpu.make_async_copy(held.at[:, :, cut], out.at[:, :, cut], done.at[piece])
        copy.start()
        copies.append(copy)
    for copy in copies:
        copy.wait()


def shards(spectra, pupils, zone_of, density, assignment, weights):
    devices = lax.axis_size("tile")
    sources = pupils.shape[1]
    scalars = pl.BlockSpec(memory_space=pltpu.SMEM)
    blocks = pl.BlockSpec(memory_space=pltpu.VMEM)
    params = pltpu.CompilerParams(vmem_limit_bytes=VMEM_LIMIT)

    hbm = pl.BlockSpec(memory_space=pltpu.HBM)
    tables = [assignment, zone_of, density, weights]
    laid, assignment, zone_of, density, weights = pl.pallas_call(
        layout_kernel,
        out_shape=[jax.ShapeDtypeStruct((devices, 12, 8, K), jnp.bfloat16)] + [pltpu.SMEM(x.shape, x.dtype) for x in tables],
        in_specs=[hbm] * 6,
        out_specs=[blocks] + [scalars] * 4,
        scratch_shapes=[pltpu.SemaphoreType.DMA((16,))],
        compiler_params=params,
        name="layout",
    )(
        pltpu.with_memory_space_constraint(pupils.reshape(sources, 2, devices, 8, K), pltpu.HBM),
        pltpu.with_memory_space_constraint(spectra.reshape(2, 2, devices, 8, K), pltpu.HBM),
        *(pltpu.with_memory_space_constraint(x, pltpu.HBM) for x in tables),
    )
    held = lax.all_to_all(laid.reshape(devices, 96, K), "tile", 0, 0, tiled=True)

    products = pl.pallas_call(
        product_kernel,
        out_shape=jax.ShapeDtypeStruct((devices, 2 * sources * 16, K), jnp.bfloat16),
        in_specs=[scalars] * 3 + [blocks],
        out_specs=blocks,
        compiler_params=params,
        name="products",
    )(assignment, zone_of, density, held)
    products = lax.all_to_all(products, "tile", 0, 0, tiled=True)

    image = pl.pallas_call(
        image_kernel,
        out_shape=jax.ShapeDtypeStruct((ROWS // 4, 8, WIDE), jnp.bfloat16),
        in_specs=[scalars] + [blocks] * 3,
        out_specs=blocks,
        compiler_params=params,
        name="images",
    )(weights, products, jnp.asarray(sample_table()), jnp.asarray(row_tables()))
    parts = lax.all_to_all(image, "src", 0, 0, tiled=True)

    return pl.pallas_call(
        finish_kernel,
        out_shape=jax.ShapeDtypeStruct((4, 2, NPIX), jnp.float32),
        in_specs=[blocks] * 2,
        out_specs=hbm,
        scratch_shapes=[pltpu.VMEM((4, 2, NPIX), jnp.float32), pltpu.SemaphoreType.DMA((4,))],
        compiler_params=params,
        name="finish",
    )(parts, jnp.asarray(interpolation_table()))


def solution(mesh):
    return jax.shard_map(
        shards,
        mesh=mesh,
        in_specs=(
            P("tile", None, None, None),
            P("tile", "src", None, None, None),
            P(),
            P(),
            P(),
            P("src"),
        ),
        out_specs=P("src", "tile", None),
        check_vma=False,
    )
```

```python
import math

import jax
import jax.numpy as jnp
import ml_dtypes
import numpy as np
from jax import lax
from jax.experimental import pallas as pl
from jax.experimental.pallas import tpu as pltpu
from jax.sharding import PartitionSpec as P

K = 128
NPIX = 2048
ROWS = 128
SAMPLES = 255
OFFSET = 0.24825
WIDE = 256
VMEM_LIMIT = 48 * 1024 * 1024


def sample_table():
    freq = np.arange(K) - K // 2
    point = np.arange(SAMPLES) + OFFSET
    angle = freq[:, None] * point[None, :] * (2.0 * math.pi / SAMPLES)
    table = np.zeros((2, K, 2, WIDE))
    table[0, :, 0, :SAMPLES] = np.cos(angle)
    table[0, :, 1, :SAMPLES] = np.sin(angle)
    table[1, :, 0, :SAMPLES] = -np.sin(angle)
    table[1, :, 1, :SAMPLES] = np.cos(angle)
    return table.reshape(2 * K, 2 * WIDE).astype(ml_dtypes.bfloat16)


def row_tables():
    freq = np.arange(K) - K // 2
    place = np.arange(ROWS)
    group, lane = place // 8, place % 8
    even = lane % 2 == 0
    first = np.where(even, 8 * group + lane // 2, 8 * group + 4 + lane // 2)
    second = np.where(even, 8 * group + 4 + lane // 2, 8 * group + lane // 2)
    out = []
    for order in (first, second):
        phase = np.mod(order[:, None] * freq[None, :], NPIX) * (2.0 * math.pi / NPIX)
        cos, sin = np.cos(phase), np.sin(phase)
        out.append(np.block([[cos, -sin], [sin, cos]]))
    return np.stack(out).astype(ml_dtypes.bfloat16)


def interpolation_table():
    theta = 2.0 * math.pi * (np.arange(NPIX)[None, :] / NPIX - (np.arange(SAMPLES)[:, None] + OFFSET) / SAMPLES)
    half = np.sin(theta / 2)
    safe = np.where(np.abs(half) < 1e-12, 1.0, half)
    kernel = np.where(np.abs(half) < 1e-12, 1.0, np.sin(SAMPLES * theta / 2) / (SAMPLES * safe))
    table = np.zeros((WIDE, NPIX))
    table[:SAMPLES] = kernel
    rounded = table.astype(ml_dtypes.bfloat16)
    missing = 1.0 - rounded.astype(np.float64).sum(0, keepdims=True)
    return rounded, missing.astype(np.float32)


def layout_kernel(pupils, spectra, assignment, zone_of, density, weights, out, tiles, zones, levels, shares, done):
    copies = [
        pltpu.make_async_copy(assignment, tiles, done.at[12]),
        pltpu.make_async_copy(zone_of, zones, done.at[13]),
        pltpu.make_async_copy(density, levels, done.at[14]),
        pltpu.make_async_copy(weights, shares, done.at[15]),
    ]
    for piece in range(12):
        source = pupils.at[piece // 2, piece % 2] if piece < 8 else spectra.at[(piece - 8) // 2, piece % 2]
        copies.append(pltpu.make_async_copy(source, out.at[:, piece], done.at[piece]))
    for copy in copies:
        copy.start()
    for copy in copies:
        copy.wait()


def product_kernel(assignment, zone_of, density, held, out):
    slots = assignment.shape[0]
    per_device = slots // out.shape[0]
    sources = 4
    freq = lax.broadcasted_iota(jnp.int32, (8, K), 0) + lax.axis_index("tile") * 8 - K // 2
    distance = jnp.abs(freq) * 8
    for slot in range(slots):
        tile = assignment[slot]
        zone = zone_of[tile]
        keep = (distance < density[tile] * K).astype(jnp.float32)
        pupil = held[zone, 0:64, :].astype(jnp.float32).reshape(sources, 2, 8, K)
        start = pl.multiple_of(64 + 16 * (tile % 2), 16)
        mask = held[tile // 2, pl.ds(start, 16), :].astype(jnp.float32).reshape(2, 8, K) * keep
        real = pupil[:, 0] * mask[0] - pupil[:, 1] * mask[1]
        imag = pupil[:, 0] * mask[1] + pupil[:, 1] * mask[0]
        both = jnp.stack([real.reshape(2, 16, K), imag.reshape(2, 16, K)], 1).reshape(64, K)
        first = 64 * (slot % per_device)
        out[slot // per_device, first : first + 64, :] = both.astype(jnp.bfloat16)


def image_kernel(weights, products, columns, rows, out):
    stacked = []
    for piece in range(4):
        real = products[:, 32 * piece : 32 * piece + 16, :].reshape(2 * K, K)
        imag = products[:, 32 * piece + 16 : 32 * piece + 32, :].reshape(2 * K, K)
        stacked.append(jnp.concatenate([real, imag], 1))
    halves = jnp.dot(jnp.concatenate(stacked, 0), columns[...], preferred_element_type=jnp.float32)
    halves = halves.reshape(2, 2, K // 8, 2, 8, 2 * WIDE)
    images = []
    for slot in range(2):
        sides = []
        for source in range(4):
            half = halves[slot, source // 2, :, source % 2].reshape(K, 2 * WIDE).astype(jnp.bfloat16)
            sides.append(jnp.concatenate([half[:, :WIDE], half[:, WIDE:]], 0))
        field = jnp.dot(rows[slot], jnp.concatenate(sides, 1), preferred_element_type=jnp.float32)
        power = field[:ROWS] * field[:ROWS] + field[ROWS:] * field[ROWS:]
        total = jnp.zeros((ROWS, WIDE), jnp.float32)
        for source in range(4):
            total = total + weights[source].astype(jnp.float32) * power[:, source * WIDE : (source + 1) * WIDE]
        images.append(total)
    weight_sum = weights[0] + weights[1] + weights[2] + weights[3]
    last = lax.broadcasted_iota(jnp.int32, (ROWS, WIDE), 1) == SAMPLES
    even = lax.broadcasted_iota(jnp.int32, (ROWS, WIDE), 0) % 2 == 0
    first = jnp.where(last, weight_sum.astype(jnp.float32), images[0])
    second = jnp.where(last, weight_sum.astype(jnp.float32), images[1])
    lower = jnp.where(even, first, second).reshape(ROWS // 8, 8, WIDE)
    upper = jnp.where(even, pltpu.roll(first, ROWS - 1, 0), pltpu.roll(second, 1, 0)).reshape(ROWS // 8, 8, WIDE)
    out[...] = jnp.stack([lower, upper], 1).reshape(ROWS // 4, 8, WIDE).astype(out.dtype)


def finish_kernel(parts, table, missing, out, held, done):
    summed = jnp.sum(parts[...].astype(jnp.float32), 0)
    total = summed[:, SAMPLES:]
    coarse = summed.astype(jnp.bfloat16)
    fine = (summed - coarse.astype(jnp.float32)).astype(jnp.bfloat16)
    both = jnp.concatenate([coarse, fine], 0)
    inside = lax.broadcasted_iota(jnp.int32, summed.shape, 1) < SAMPLES
    mean = jnp.sum(jnp.where(inside, summed, 0.0), 1, keepdims=True) * (1.0 / SAMPLES)
    copies = []
    width = NPIX // 4
    for piece in range(4):
        cut = pl.ds(width * piece, width)
        spread = jnp.dot(both, table[:, cut], preferred_element_type=jnp.float32)
        result = (mean * missing[:, cut] + (spread[:8] + spread[8:])) / total
        for row in range(4):
            held[row, :, cut] = result[2 * row : 2 * row + 2]
        copy = pltpu.make_async_copy(held.at[:, :, cut], out.at[:, :, cut], done.at[piece])
        copy.start()
        copies.append(copy)
    for copy in copies:
        copy.wait()


def shards(spectra, pupils, zone_of, density, assignment, weights):
    devices = lax.axis_size("tile")
    sources = pupils.shape[1]
    scalars = pl.BlockSpec(memory_space=pltpu.SMEM)
    blocks = pl.BlockSpec(memory_space=pltpu.VMEM)
    params = pltpu.CompilerParams(vmem_limit_bytes=VMEM_LIMIT)

    hbm = pl.BlockSpec(memory_space=pltpu.HBM)
    tables = [assignment, zone_of, density, weights]
    laid, assignment, zone_of, density, weights = pl.pallas_call(
        layout_kernel,
        out_shape=[jax.ShapeDtypeStruct((devices, 12, 8, K), jnp.bfloat16)] + [pltpu.SMEM(x.shape, x.dtype) for x in tables],
        in_specs=[hbm] * 6,
        out_specs=[blocks] + [scalars] * 4,
        scratch_shapes=[pltpu.SemaphoreType.DMA((16,))],
        compiler_params=params,
        name="layout",
    )(
        pltpu.with_memory_space_constraint(pupils.reshape(sources, 2, devices, 8, K), pltpu.HBM),
        pltpu.with_memory_space_constraint(spectra.reshape(2, 2, devices, 8, K), pltpu.HBM),
        *(pltpu.with_memory_space_constraint(x, pltpu.HBM) for x in tables),
    )
    held = lax.all_to_all(laid.reshape(devices, 96, K), "tile", 0, 0, tiled=True)

    products = pl.pallas_call(
        product_kernel,
        out_shape=jax.ShapeDtypeStruct((devices, 2 * sources * 16, K), jnp.bfloat16),
        in_specs=[scalars] * 3 + [blocks],
        out_specs=blocks,
        compiler_params=params,
        name="products",
    )(assignment, zone_of, density, held)
    products = lax.all_to_all(products, "tile", 0, 0, tiled=True)

    image = pl.pallas_call(
        image_kernel,
        out_shape=jax.ShapeDtypeStruct((ROWS // 4, 8, WIDE), jnp.bfloat16),
        in_specs=[scalars] + [blocks] * 3,
        out_specs=blocks,
        compiler_params=params,
        name="images",
    )(weights, products, jnp.asarray(sample_table()), jnp.asarray(row_tables()))
    parts = lax.all_to_all(image, "src", 0, 0, tiled=True)

    return pl.pallas_call(
        finish_kernel,
        out_shape=jax.ShapeDtypeStruct((4, 2, NPIX), jnp.float32),
        in_specs=[blocks] * 3,
        out_specs=hbm,
        scratch_shapes=[pltpu.VMEM((4, 2, NPIX), jnp.float32), pltpu.SemaphoreType.DMA((4,))],
        compiler_params=params,
        name="finish",
    )(parts, *(jnp.asarray(x) for x in interpolation_table()))


def solution(mesh):
    return jax.shard_map(
        shards,
        mesh=mesh,
        in_specs=(
            P("tile", None, None, None),
            P("tile", "src", None, None, None),
            P(),
            P(),
            P(),
            P("src"),
        ),
        out_specs=P("src", "tile", None),
        check_vma=False,
    )
```

```python
import math

import jax
import jax.numpy as jnp
import ml_dtypes
import numpy as np
from jax import lax
from jax.experimental import pallas as pl
from jax.experimental.pallas import tpu as pltpu
from jax.sharding import PartitionSpec as P

K = 128
NPIX = 2048
ROWS = 128
SAMPLES = 255
OFFSET = 0.24825
WIDE = 256
VMEM_LIMIT = 48 * 1024 * 1024


def sample_table():
    freq = np.arange(K) - K // 2
    point = np.arange(SAMPLES) + OFFSET
    angle = freq[:, None] * point[None, :] * (2.0 * math.pi / SAMPLES)
    table = np.zeros((2, K, 2, WIDE))
    table[0, :, 0, :SAMPLES] = np.cos(angle)
    table[0, :, 1, :SAMPLES] = np.sin(angle)
    table[1, :, 0, :SAMPLES] = -np.sin(angle)
    table[1, :, 1, :SAMPLES] = np.cos(angle)
    return table.reshape(2 * K, 2 * WIDE).astype(ml_dtypes.bfloat16)


def row_tables():
    freq = np.arange(K) - K // 2
    place = np.arange(ROWS)
    group, lane = place // 8, place % 8
    even = lane % 2 == 0
    first = np.where(even, 8 * group + lane // 2, 8 * group + 4 + lane // 2)
    second = np.where(even, 8 * group + 4 + lane // 2, 8 * group + lane // 2)
    out = []
    for order in (first, second):
        phase = np.mod(order[:, None] * freq[None, :], NPIX) * (2.0 * math.pi / NPIX)
        cos, sin = np.cos(phase), np.sin(phase)
        out.append(np.block([[cos, -sin], [sin, cos]]))
    return np.stack(out).astype(ml_dtypes.bfloat16)


def interpolation_table():
    theta = 2.0 * math.pi * (np.arange(NPIX)[None, :] / NPIX - (np.arange(SAMPLES)[:, None] + OFFSET) / SAMPLES)
    half = np.sin(theta / 2)
    safe = np.where(np.abs(half) < 1e-12, 1.0, half)
    kernel = np.where(np.abs(half) < 1e-12, 1.0, np.sin(SAMPLES * theta / 2) / (SAMPLES * safe))
    table = np.zeros((WIDE, NPIX))
    table[:SAMPLES] = kernel
    rounded = table.astype(ml_dtypes.bfloat16)
    missing = 1.0 - rounded.astype(np.float64).sum(0, keepdims=True)
    return rounded, missing.astype(np.float32)


def layout_kernel(pupils, spectra, assignment, zone_of, density, weights, out, tiles, zones, levels, shares, done):
    copies = [
        pltpu.make_async_copy(assignment, tiles, done.at[12]),
        pltpu.make_async_copy(zone_of, zones, done.at[13]),
        pltpu.make_async_copy(density, levels, done.at[14]),
        pltpu.make_async_copy(weights, shares, done.at[15]),
    ]
    for piece in range(12):
        source = pupils.at[piece // 2, piece % 2] if piece < 8 else spectra.at[(piece - 8) // 2, piece % 2]
        copies.append(pltpu.make_async_copy(source, out.at[:, piece], done.at[piece]))
    for copy in copies:
        copy.start()
    for copy in copies:
        copy.wait()


def product_kernel(assignment, zone_of, density, held, out):
    slots = assignment.shape[0]
    per_device = slots // out.shape[0]
    sources = 4
    freq = lax.broadcasted_iota(jnp.int32, (8, K), 0) + lax.axis_index("tile") * 8 - K // 2
    distance = jnp.abs(freq) * 8
    for slot in range(slots):
        tile = assignment[slot]
        zone = zone_of[tile]
        keep = (distance < density[tile] * K).astype(jnp.float32)
        pupil = held[zone, 0:64, :].astype(jnp.float32).reshape(sources, 2, 8, K)
        start = pl.multiple_of(64 + 16 * (tile % 2), 16)
        mask = held[tile // 2, pl.ds(start, 16), :].astype(jnp.float32).reshape(2, 8, K) * keep
        real = pupil[:, 0] * mask[0] - pupil[:, 1] * mask[1]
        imag = pupil[:, 0] * mask[1] + pupil[:, 1] * mask[0]
        both = jnp.stack([real.reshape(2, 16, K), imag.reshape(2, 16, K)], 1).reshape(64, K)
        first = 64 * (slot % per_device)
        out[slot // per_device, first : first + 64, :] = both.astype(jnp.bfloat16)


def image_kernel(weights, products, columns, rows, out):
    stacked = []
    for piece in range(4):
        real = products[:, 32 * piece : 32 * piece + 16, :].reshape(2 * K, K)
        imag = products[:, 32 * piece + 16 : 32 * piece + 32, :].reshape(2 * K, K)
        stacked.append(jnp.concatenate([real, imag], 1))
    halves = jnp.dot(jnp.concatenate(stacked, 0), columns[...], preferred_element_type=jnp.float32)
    halves = halves.reshape(2, 2, K // 8, 2, 8, 2 * WIDE)
    images = []
    for slot in range(2):
        sides = []
        for source in range(4):
            half = halves[slot, source // 2, :, source % 2].reshape(K, 2 * WIDE).astype(jnp.bfloat16)
            sides.append(jnp.concatenate([half[:, :WIDE], half[:, WIDE:]], 0))
        field = jnp.dot(rows[slot], jnp.concatenate(sides, 1), preferred_element_type=jnp.float32)
        power = field[:ROWS] * field[:ROWS] + field[ROWS:] * field[ROWS:]
        total = jnp.zeros((ROWS, WIDE), jnp.float32)
        for source in range(4):
            total = total + weights[source].astype(jnp.float32) * power[:, source * WIDE : (source + 1) * WIDE]
        images.append(total)
    weight_sum = weights[0] + weights[1] + weights[2] + weights[3]
    last = lax.broadcasted_iota(jnp.int32, (ROWS, WIDE), 1) == SAMPLES
    even = lax.broadcasted_iota(jnp.int32, (ROWS, WIDE), 0) % 2 == 0
    first = jnp.where(last, weight_sum.astype(jnp.float32), images[0])
    second = jnp.where(last, weight_sum.astype(jnp.float32), images[1])
    lower = jnp.where(even, first, second).reshape(ROWS // 8, 8, WIDE)
    upper = jnp.where(even, pltpu.roll(first, ROWS - 1, 0), pltpu.roll(second, 1, 0)).reshape(ROWS // 8, 8, WIDE)
    out[...] = jnp.stack([lower, upper], 1).reshape(ROWS // 4, 8, WIDE).astype(out.dtype)


def finish_kernel(parts, table, missing, out):
    summed = jnp.sum(parts[...].astype(jnp.float32), 0)
    total = summed[:, SAMPLES:]
    coarse = summed.astype(jnp.bfloat16)
    fine = (summed - coarse.astype(jnp.float32)).astype(jnp.bfloat16)
    both = jnp.concatenate([coarse, fine], 0)
    inside = lax.broadcasted_iota(jnp.int32, summed.shape, 1) < SAMPLES
    mean = jnp.sum(jnp.where(inside, summed, 0.0), 1, keepdims=True) * (1.0 / SAMPLES)
    spread = jnp.dot(both, table[...], preferred_element_type=jnp.float32)
    result = (mean * missing[...] + (spread[:8] + spread[8:])) / total
    for row in range(out.shape[0]):
        out[row] = result[2 * row : 2 * row + 2]


def shards(spectra, pupils, zone_of, density, assignment, weights):
    devices = lax.axis_size("tile")
    sources = pupils.shape[1]
    scalars = pl.BlockSpec(memory_space=pltpu.SMEM)
    blocks = pl.BlockSpec(memory_space=pltpu.VMEM)
    params = pltpu.CompilerParams(vmem_limit_bytes=VMEM_LIMIT)

    hbm = pl.BlockSpec(memory_space=pltpu.HBM)
    tables = [assignment, zone_of, density, weights]
    laid, assignment, zone_of, density, weights = pl.pallas_call(
        layout_kernel,
        out_shape=[jax.ShapeDtypeStruct((devices, 12, 8, K), jnp.bfloat16)] + [pltpu.SMEM(x.shape, x.dtype) for x in tables],
        in_specs=[hbm] * 6,
        out_specs=[blocks] + [scalars] * 4,
        scratch_shapes=[pltpu.SemaphoreType.DMA((16,))],
        compiler_params=params,
        name="layout",
    )(
        pltpu.with_memory_space_constraint(pupils.reshape(sources, 2, devices, 8, K), pltpu.HBM),
        pltpu.with_memory_space_constraint(spectra.reshape(2, 2, devices, 8, K), pltpu.HBM),
        *(pltpu.with_memory_space_constraint(x, pltpu.HBM) for x in tables),
    )
    held = lax.all_to_all(laid.reshape(devices, 96, K), "tile", 0, 0, tiled=True)

    products = pl.pallas_call(
        product_kernel,
        out_shape=jax.ShapeDtypeStruct((devices, 2 * sources * 16, K), jnp.bfloat16),
        in_specs=[scalars] * 3 + [blocks],
        out_specs=blocks,
        compiler_params=params,
        name="products",
    )(assignment, zone_of, density, held)
    products = lax.all_to_all(products, "tile", 0, 0, tiled=True)

    image = pl.pallas_call(
        image_kernel,
        out_shape=jax.ShapeDtypeStruct((ROWS // 4, 8, WIDE), jnp.bfloat16),
        in_specs=[scalars] + [blocks] * 3,
        out_specs=blocks,
        compiler_params=params,
        name="images",
    )(weights, products, jnp.asarray(sample_table()), jnp.asarray(row_tables()))
    parts = lax.all_to_all(image, "src", 0, 0, tiled=True)

    return pl.pallas_call(
        finish_kernel,
        out_shape=jax.ShapeDtypeStruct((4, 2, NPIX), jnp.float32),
        in_specs=[blocks] * 3,
        out_specs=blocks,
        compiler_params=params,
        name="finish",
    )(parts, *(jnp.asarray(x) for x in interpolation_table()))


def solution(mesh):
    return jax.shard_map(
        shards,
        mesh=mesh,
        in_specs=(
            P("tile", None, None, None),
            P("tile", "src", None, None, None),
            P(),
            P(),
            P(),
            P("src"),
        ),
        out_specs=P("src", "tile", None),
        check_vma=False,
    )
```

```python
import math

import jax
import jax.numpy as jnp
import ml_dtypes
import numpy as np
from jax import lax
from jax.experimental import pallas as pl
from jax.experimental.pallas import tpu as pltpu
from jax.sharding import PartitionSpec as P

K = 128
NPIX = 2048
ROWS = 128
SAMPLES = 255
OFFSET = 0.24825
WIDE = 256
VMEM_LIMIT = 48 * 1024 * 1024


def sample_table():
    freq = np.arange(K) - K // 2
    point = np.arange(SAMPLES) + OFFSET
    angle = freq[:, None] * point[None, :] * (2.0 * math.pi / SAMPLES)
    table = np.zeros((2, K, 2, WIDE))
    table[0, :, 0, :SAMPLES] = np.cos(angle)
    table[0, :, 1, :SAMPLES] = np.sin(angle)
    table[1, :, 0, :SAMPLES] = -np.sin(angle)
    table[1, :, 1, :SAMPLES] = np.cos(angle)
    return table.reshape(2 * K, 2 * WIDE).astype(ml_dtypes.bfloat16)


def row_tables():
    freq = np.arange(K) - K // 2
    place = np.arange(ROWS)
    group, lane = place // 8, place % 8
    even = lane % 2 == 0
    first = np.where(even, 8 * group + lane // 2, 8 * group + 4 + lane // 2)
    second = np.where(even, 8 * group + 4 + lane // 2, 8 * group + lane // 2)
    out = []
    for order in (first, second):
        phase = np.mod(order[:, None] * freq[None, :], NPIX) * (2.0 * math.pi / NPIX)
        cos, sin = np.cos(phase), np.sin(phase)
        out.append(np.block([[cos, -sin], [sin, cos]]))
    return np.stack(out).astype(ml_dtypes.bfloat16)


def interpolation_table():
    theta = 2.0 * math.pi * (np.arange(NPIX)[None, :] / NPIX - (np.arange(SAMPLES)[:, None] + OFFSET) / SAMPLES)
    half = np.sin(theta / 2)
    safe = np.where(np.abs(half) < 1e-12, 1.0, half)
    kernel = np.where(np.abs(half) < 1e-12, 1.0, np.sin(SAMPLES * theta / 2) / (SAMPLES * safe))
    table = np.zeros((WIDE, NPIX))
    table[:SAMPLES] = kernel
    rounded = table.astype(ml_dtypes.bfloat16)
    missing = 1.0 - rounded.astype(np.float64).sum(0, keepdims=True)
    return rounded, missing.astype(np.float32)


def layout_kernel(pupils, spectra, assignment, zone_of, density, weights, out, tiles, zones, levels, shares, done):
    copies = [
        pltpu.make_async_copy(assignment, tiles, done.at[12]),
        pltpu.make_async_copy(zone_of, zones, done.at[13]),
        pltpu.make_async_copy(density, levels, done.at[14]),
        pltpu.make_async_copy(weights, shares, done.at[15]),
    ]
    for piece in range(12):
        source = pupils.at[piece // 2, piece % 2] if piece < 8 else spectra.at[(piece - 8) // 2, piece % 2]
        copies.append(pltpu.make_async_copy(source, out.at[:, piece], done.at[piece]))
    for copy in copies:
        copy.start()
    for copy in copies:
        copy.wait()


def product_kernel(assignment, zone_of, density, held, out):
    slots = assignment.shape[0]
    per_device = slots // out.shape[0]
    sources = 4
    freq = lax.broadcasted_iota(jnp.int32, (8, K), 0) + lax.axis_index("tile") * 8 - K // 2
    distance = jnp.abs(freq) * 8
    for slot in range(slots):
        tile = assignment[slot]
        zone = zone_of[tile]
        keep = (distance < density[tile] * K).astype(jnp.float32)
        pupil = held[zone, 0:64, :].astype(jnp.float32).reshape(sources, 2, 8, K)
        start = pl.multiple_of(64 + 16 * (tile % 2), 16)
        mask = held[tile // 2, pl.ds(start, 16), :].astype(jnp.float32).reshape(2, 8, K) * keep
        real = pupil[:, 0] * mask[0] - pupil[:, 1] * mask[1]
        imag = pupil[:, 0] * mask[1] + pupil[:, 1] * mask[0]
        both = jnp.stack([real.reshape(2, 16, K), imag.reshape(2, 16, K)], 1).reshape(64, K)
        first = 64 * (slot % per_device)
        out[slot // per_device, first : first + 64, :] = both.astype(jnp.bfloat16)


def image_kernel(weights, products, columns, rows, out):
    stacked = []
    for piece in range(4):
        real = products[:, 32 * piece : 32 * piece + 16, :].reshape(2 * K, K)
        imag = products[:, 32 * piece + 16 : 32 * piece + 32, :].reshape(2 * K, K)
        stacked.append(jnp.concatenate([real, imag], 1))
    halves = jnp.dot(jnp.concatenate(stacked, 0), columns[...], preferred_element_type=jnp.float32)
    halves = halves.reshape(2, 2, K // 8, 2, 8, 2 * WIDE)
    images = []
    for slot in range(2):
        sides = []
        for source in range(4):
            half = halves[slot, source // 2, :, source % 2].reshape(K, 2 * WIDE).astype(jnp.bfloat16)
            sides.append(jnp.concatenate([half[:, :WIDE], half[:, WIDE:]], 0))
        field = jnp.dot(rows[slot], jnp.concatenate(sides, 1), preferred_element_type=jnp.float32)
        power = field[:ROWS] * field[:ROWS] + field[ROWS:] * field[ROWS:]
        total = jnp.zeros((ROWS, WIDE), jnp.float32)
        for source in range(4):
            total = total + weights[source].astype(jnp.float32) * power[:, source * WIDE : (source + 1) * WIDE]
        images.append(total)
    weight_sum = weights[0] + weights[1] + weights[2] + weights[3]
    last = lax.broadcasted_iota(jnp.int32, (ROWS, WIDE), 1) == SAMPLES
    even = lax.broadcasted_iota(jnp.int32, (ROWS, WIDE), 0) % 2 == 0
    first = jnp.where(last, weight_sum.astype(jnp.float32), images[0])
    second = jnp.where(last, weight_sum.astype(jnp.float32), images[1])
    lower = jnp.where(even, first, second).reshape(ROWS // 8, 8, WIDE)
    upper = jnp.where(even, pltpu.roll(first, ROWS - 1, 0), pltpu.roll(second, 1, 0)).reshape(ROWS // 8, 8, WIDE)
    rows_of = jnp.stack([lower, upper], 1).reshape(ROWS // 4, 8, WIDE)
    out[...] = jnp.concatenate([rows_of[:, :, :K], rows_of[:, :, K:]], 1).astype(out.dtype)


def finish_kernel(parts, table, missing, out):
    halves = jnp.sum(parts[...].astype(jnp.float32), 0)
    summed = jnp.concatenate([halves[:8], halves[8:]], 1)
    total = summed[:, SAMPLES:]
    coarse = summed.astype(jnp.bfloat16)
    fine = (summed - coarse.astype(jnp.float32)).astype(jnp.bfloat16)
    both = jnp.concatenate([coarse, fine], 0)
    inside = lax.broadcasted_iota(jnp.int32, summed.shape, 1) < SAMPLES
    mean = jnp.sum(jnp.where(inside, summed, 0.0), 1, keepdims=True) * (1.0 / SAMPLES)
    spread = jnp.dot(both, table[...], preferred_element_type=jnp.float32)
    result = (mean * missing[...] + (spread[:8] + spread[8:])) / total
    for row in range(out.shape[0]):
        out[row] = result[2 * row : 2 * row + 2]


def shards(spectra, pupils, zone_of, density, assignment, weights):
    devices = lax.axis_size("tile")
    sources = pupils.shape[1]
    scalars = pl.BlockSpec(memory_space=pltpu.SMEM)
    blocks = pl.BlockSpec(memory_space=pltpu.VMEM)
    params = pltpu.CompilerParams(vmem_limit_bytes=VMEM_LIMIT)

    hbm = pl.BlockSpec(memory_space=pltpu.HBM)
    tables = [assignment, zone_of, density, weights]
    laid, assignment, zone_of, density, weights = pl.pallas_call(
        layout_kernel,
        out_shape=[jax.ShapeDtypeStruct((devices, 12, 8, K), jnp.bfloat16)] + [pltpu.SMEM(x.shape, x.dtype) for x in tables],
        in_specs=[hbm] * 6,
        out_specs=[blocks] + [scalars] * 4,
        scratch_shapes=[pltpu.SemaphoreType.DMA((16,))],
        compiler_params=params,
        name="layout",
    )(
        pltpu.with_memory_space_constraint(pupils.reshape(sources, 2, devices, 8, K), pltpu.HBM),
        pltpu.with_memory_space_constraint(spectra.reshape(2, 2, devices, 8, K), pltpu.HBM),
        *(pltpu.with_memory_space_constraint(x, pltpu.HBM) for x in tables),
    )
    held = lax.all_to_all(laid.reshape(devices, 96, K), "tile", 0, 0, tiled=True)

    products = pl.pallas_call(
        product_kernel,
        out_shape=jax.ShapeDtypeStruct((devices, 2 * sources * 16, K), jnp.bfloat16),
        in_specs=[scalars] * 3 + [blocks],
        out_specs=blocks,
        compiler_params=params,
        name="products",
    )(assignment, zone_of, density, held)
    products = lax.all_to_all(products, "tile", 0, 0, tiled=True)

    image = pl.pallas_call(
        image_kernel,
        out_shape=jax.ShapeDtypeStruct((ROWS // 4, 16, K), jnp.bfloat16),
        in_specs=[scalars] + [blocks] * 3,
        out_specs=blocks,
        compiler_params=params,
        name="images",
    )(weights, products, jnp.asarray(sample_table()), jnp.asarray(row_tables()))
    parts = lax.all_to_all(image, "src", 0, 0, tiled=True)

    return pl.pallas_call(
        finish_kernel,
        out_shape=jax.ShapeDtypeStruct((4, 2, NPIX), jnp.float32),
        in_specs=[blocks] * 3,
        out_specs=blocks,
        compiler_params=params,
        name="finish",
    )(parts, *(jnp.asarray(x) for x in interpolation_table()))


def solution(mesh):
    return jax.shard_map(
        shards,
        mesh=mesh,
        in_specs=(
            P("tile", None, None, None),
            P("tile", "src", None, None, None),
            P(),
            P(),
            P(),
            P("src"),
        ),
        out_specs=P("src", "tile", None),
        check_vma=False,
    )
```

```python
import math

import jax
import jax.numpy as jnp
import ml_dtypes
import numpy as np
from jax import lax
from jax.experimental import pallas as pl
from jax.experimental.pallas import tpu as pltpu
from jax.sharding import PartitionSpec as P

K = 128
NPIX = 2048
ROWS = 128
SAMPLES = 255
OFFSET = 0.24825
WIDE = 256
VMEM_LIMIT = 48 * 1024 * 1024


def sample_table():
    freq = np.arange(K) - K // 2
    point = np.arange(SAMPLES) + OFFSET
    angle = freq[:, None] * point[None, :] * (2.0 * math.pi / SAMPLES)
    table = np.zeros((2, K, 2, WIDE))
    table[0, :, 0, :SAMPLES] = np.cos(angle)
    table[0, :, 1, :SAMPLES] = np.sin(angle)
    table[1, :, 0, :SAMPLES] = -np.sin(angle)
    table[1, :, 1, :SAMPLES] = np.cos(angle)
    return table.reshape(2 * K, 2 * WIDE).astype(ml_dtypes.bfloat16)


def row_tables():
    freq = np.arange(K) - K // 2
    place = np.arange(ROWS)
    group, lane = place // 8, place % 8
    even = lane % 2 == 0
    first = np.where(even, 8 * group + lane // 2, 8 * group + 4 + lane // 2)
    second = np.where(even, 8 * group + 4 + lane // 2, 8 * group + lane // 2)
    out = []
    for order in (first, second):
        phase = np.mod(order[:, None] * freq[None, :], NPIX) * (2.0 * math.pi / NPIX)
        cos, sin = np.cos(phase), np.sin(phase)
        out.append(np.block([[cos, -sin], [sin, cos]]))
    return np.stack(out).astype(ml_dtypes.bfloat16)


def interpolation_table():
    theta = 2.0 * math.pi * (np.arange(NPIX)[None, :] / NPIX - (np.arange(SAMPLES)[:, None] + OFFSET) / SAMPLES)
    half = np.sin(theta / 2)
    safe = np.where(np.abs(half) < 1e-12, 1.0, half)
    kernel = np.where(np.abs(half) < 1e-12, 1.0, np.sin(SAMPLES * theta / 2) / (SAMPLES * safe))
    table = np.zeros((WIDE, NPIX))
    table[:SAMPLES] = kernel
    rounded = table.astype(ml_dtypes.bfloat16)
    missing = 1.0 - rounded.astype(np.float64).sum(0, keepdims=True)
    return rounded, missing.astype(np.float32)


def layout_kernel(pupils, spectra, assignment, zone_of, density, weights, out, tiles, zones, levels, shares, done):
    copies = [
        pltpu.make_async_copy(assignment, tiles, done.at[12]),
        pltpu.make_async_copy(zone_of, zones, done.at[13]),
        pltpu.make_async_copy(density, levels, done.at[14]),
        pltpu.make_async_copy(weights, shares, done.at[15]),
    ]
    for piece in range(12):
        source = pupils.at[piece // 2, piece % 2] if piece < 8 else spectra.at[(piece - 8) // 2, piece % 2]
        copies.append(pltpu.make_async_copy(source, out.at[:, piece], done.at[piece]))
    for copy in copies:
        copy.start()
    for copy in copies:
        copy.wait()


def product_kernel(assignment, zone_of, density, held, out):
    slots = assignment.shape[0]
    per_device = slots // out.shape[0]
    sources = 4
    freq = lax.broadcasted_iota(jnp.int32, (8, K), 0) + lax.axis_index("tile") * 8 - K // 2
    distance = jnp.abs(freq) * 8
    for slot in range(slots):
        tile = assignment[slot]
        zone = zone_of[tile]
        keep = (distance < density[tile] * K).astype(jnp.float32)
        pupil = held[zone, 0:64, :].astype(jnp.float32).reshape(sources, 2, 8, K)
        start = pl.multiple_of(64 + 16 * (tile % 2), 16)
        mask = held[tile // 2, pl.ds(start, 16), :].astype(jnp.float32).reshape(2, 8, K) * keep
        real = pupil[:, 0] * mask[0] - pupil[:, 1] * mask[1]
        imag = pupil[:, 0] * mask[1] + pupil[:, 1] * mask[0]
        both = jnp.stack([real.reshape(2, 16, K), imag.reshape(2, 16, K)], 1).reshape(64, K)
        first = 64 * (slot % per_device)
        out[slot // per_device, first : first + 64, :] = both.astype(jnp.bfloat16)


def image_kernel(weights, products, columns, rows, out):
    stacked = []
    for piece in range(4):
        real = products[:, 32 * piece : 32 * piece + 16, :].reshape(2 * K, K)
        imag = products[:, 32 * piece + 16 : 32 * piece + 32, :].reshape(2 * K, K)
        stacked.append(jnp.concatenate([real, imag], 1))
    halves = jnp.dot(jnp.concatenate(stacked, 0), columns[...], preferred_element_type=jnp.float32)
    halves = halves.reshape(2, 2, K // 8, 2, 8, 2 * WIDE)
    images = []
    for slot in range(2):
        sides = []
        for source in range(4):
            half = halves[slot, source // 2, :, source % 2].reshape(K, 2 * WIDE).astype(jnp.bfloat16)
            sides.append(jnp.concatenate([half[:, :WIDE], half[:, WIDE:]], 0))
        field = jnp.dot(rows[slot], jnp.concatenate(sides, 1), preferred_element_type=jnp.float32)
        power = field[:ROWS] * field[:ROWS] + field[ROWS:] * field[ROWS:]
        total = jnp.zeros((ROWS, WIDE), jnp.float32)
        for source in range(4):
            total = total + weights[source].astype(jnp.float32) * power[:, source * WIDE : (source + 1) * WIDE]
        images.append(total)
    weight_sum = weights[0] + weights[1] + weights[2] + weights[3]
    last = lax.broadcasted_iota(jnp.int32, (ROWS, WIDE), 1) == SAMPLES
    even = lax.broadcasted_iota(jnp.int32, (ROWS, WIDE), 0) % 2 == 0
    first = jnp.where(last, weight_sum.astype(jnp.float32), images[0])
    second = jnp.where(last, weight_sum.astype(jnp.float32), images[1])
    lower = jnp.where(even, first, second).reshape(ROWS // 8, 8, WIDE)
    upper = jnp.where(even, pltpu.roll(first, ROWS - 1, 0), pltpu.roll(second, 1, 0)).reshape(ROWS // 8, 8, WIDE)
    out[...] = jnp.stack([lower, upper], 1).reshape(ROWS // 4, 8, WIDE).astype(out.dtype)


def finish_kernel(parts, table, missing, out, held, done):
    summed = jnp.sum(parts[...].astype(jnp.float32), 0)
    total = summed[:, SAMPLES:]
    coarse = summed.astype(jnp.bfloat16)
    fine = (summed - coarse.astype(jnp.float32)).astype(jnp.bfloat16)
    both = jnp.concatenate([coarse, fine], 0)
    inside = lax.broadcasted_iota(jnp.int32, summed.shape, 1) < SAMPLES
    mean = jnp.sum(jnp.where(inside, summed, 0.0), 1, keepdims=True) * (1.0 / SAMPLES)
    copies = []
    width = NPIX // 2
    for piece in range(2):
        cut = pl.ds(width * piece, width)
        spread = jnp.dot(both, table[:, cut], preferred_element_type=jnp.float32)
        result = (mean * missing[:, cut] + (spread[:8] + spread[8:])) / total
        for row in range(4):
            held[row, :, cut] = result[2 * row : 2 * row + 2]
        copy = pltpu.make_async_copy(held.at[:, :, cut], out.at[:, :, cut], done.at[piece])
        copy.start()
        copies.append(copy)
    for copy in copies:
        copy.wait()


def shards(spectra, pupils, zone_of, density, assignment, weights):
    devices = lax.axis_size("tile")
    sources = pupils.shape[1]
    scalars = pl.BlockSpec(memory_space=pltpu.SMEM)
    blocks = pl.BlockSpec(memory_space=pltpu.VMEM)
    params = pltpu.CompilerParams(vmem_limit_bytes=VMEM_LIMIT)

    hbm = pl.BlockSpec(memory_space=pltpu.HBM)
    tables = [assignment, zone_of, density, weights]
    laid, assignment, zone_of, density, weights = pl.pallas_call(
        layout_kernel,
        out_shape=[jax.ShapeDtypeStruct((devices, 12, 8, K), jnp.bfloat16)] + [pltpu.SMEM(x.shape, x.dtype) for x in tables],
        in_specs=[hbm] * 6,
        out_specs=[blocks] + [scalars] * 4,
        scratch_shapes=[pltpu.SemaphoreType.DMA((16,))],
        compiler_params=params,
        name="layout",
    )(
        pltpu.with_memory_space_constraint(pupils.reshape(sources, 2, devices, 8, K), pltpu.HBM),
        pltpu.with_memory_space_constraint(spectra.reshape(2, 2, devices, 8, K), pltpu.HBM),
        *(pltpu.with_memory_space_constraint(x, pltpu.HBM) for x in tables),
    )
    held = lax.all_to_all(laid.reshape(devices, 96, K), "tile", 0, 0, tiled=True)

    products = pl.pallas_call(
        product_kernel,
        out_shape=jax.ShapeDtypeStruct((devices, 2 * sources * 16, K), jnp.bfloat16),
        in_specs=[scalars] * 3 + [blocks],
        out_specs=blocks,
        compiler_params=params,
        name="products",
    )(assignment, zone_of, density, held)
    products = lax.all_to_all(products, "tile", 0, 0, tiled=True)

    image = pl.pallas_call(
        image_kernel,
        out_shape=jax.ShapeDtypeStruct((ROWS // 4, 8, WIDE), jnp.bfloat16),
        in_specs=[scalars] + [blocks] * 3,
        out_specs=blocks,
        compiler_params=params,
        name="images",
    )(weights, products, jnp.asarray(sample_table()), jnp.asarray(row_tables()))
    parts = lax.all_to_all(image, "src", 0, 0, tiled=True)

    return pl.pallas_call(
        finish_kernel,
        out_shape=jax.ShapeDtypeStruct((4, 2, NPIX), jnp.float32),
        in_specs=[blocks] * 3,
        out_specs=hbm,
        scratch_shapes=[pltpu.VMEM((4, 2, NPIX), jnp.float32), pltpu.SemaphoreType.DMA((4,))],
        compiler_params=params,
        name="finish",
    )(parts, *(jnp.asarray(x) for x in interpolation_table()))


def solution(mesh):
    return jax.shard_map(
        shards,
        mesh=mesh,
        in_specs=(
            P("tile", None, None, None),
            P("tile", "src", None, None, None),
            P(),
            P(),
            P(),
            P("src"),
        ),
        out_specs=P("src", "tile", None),
        check_vma=False,
    )
```

```python
import math

import jax
import jax.numpy as jnp
import ml_dtypes
import numpy as np
from jax import lax
from jax.experimental import pallas as pl
from jax.experimental.pallas import tpu as pltpu
from jax.sharding import PartitionSpec as P

K = 128
NPIX = 2048
ROWS = 128
SAMPLES = 255
OFFSET = 0.24825
WIDE = 256
VMEM_LIMIT = 48 * 1024 * 1024


def sample_table():
    freq = np.arange(K) - K // 2
    point = np.arange(SAMPLES) + OFFSET
    angle = freq[:, None] * point[None, :] * (2.0 * math.pi / SAMPLES)
    table = np.zeros((2, K, 2, WIDE))
    table[0, :, 0, :SAMPLES] = np.cos(angle)
    table[0, :, 1, :SAMPLES] = np.sin(angle)
    table[1, :, 0, :SAMPLES] = -np.sin(angle)
    table[1, :, 1, :SAMPLES] = np.cos(angle)
    return table.reshape(2 * K, 2 * WIDE).astype(ml_dtypes.bfloat16)


def row_tables():
    freq = np.arange(K) - K // 2
    place = np.arange(ROWS)
    group, lane = place // 8, place % 8
    even = lane % 2 == 0
    first = np.where(even, 8 * group + lane // 2, 8 * group + 4 + lane // 2)
    second = np.where(even, 8 * group + 4 + lane // 2, 8 * group + lane // 2)
    out = []
    for order in (first, second):
        phase = np.mod(order[:, None] * freq[None, :], NPIX) * (2.0 * math.pi / NPIX)
        cos, sin = np.cos(phase), np.sin(phase)
        out.append(np.block([[cos, -sin], [sin, cos]]))
    return np.stack(out).astype(ml_dtypes.bfloat16)


def interpolation_table():
    theta = 2.0 * math.pi * (np.arange(NPIX)[None, :] / NPIX - (np.arange(SAMPLES)[:, None] + OFFSET) / SAMPLES)
    half = np.sin(theta / 2)
    safe = np.where(np.abs(half) < 1e-12, 1.0, half)
    kernel = np.where(np.abs(half) < 1e-12, 1.0, np.sin(SAMPLES * theta / 2) / (SAMPLES * safe))
    table = np.zeros((WIDE, NPIX))
    table[:SAMPLES] = kernel
    return table.astype(ml_dtypes.bfloat16)


def layout_kernel(pupils, spectra, assignment, zone_of, density, weights, out, tiles, zones, levels, shares, done):
    copies = [
        pltpu.make_async_copy(assignment, tiles, done.at[12]),
        pltpu.make_async_copy(zone_of, zones, done.at[13]),
        pltpu.make_async_copy(density, levels, done.at[14]),
        pltpu.make_async_copy(weights, shares, done.at[15]),
    ]
    for piece in range(12):
        source = pupils.at[piece // 2, piece % 2] if piece < 8 else spectra.at[(piece - 8) // 2, piece % 2]
        copies.append(pltpu.make_async_copy(source, out.at[:, piece], done.at[piece]))
    for copy in copies:
        copy.start()
    for copy in copies:
        copy.wait()


def product_kernel(assignment, zone_of, density, held, out):
    slots = assignment.shape[0]
    per_device = slots // out.shape[0]
    sources = 4
    freq = lax.broadcasted_iota(jnp.int32, (8, K), 0) + lax.axis_index("tile") * 8 - K // 2
    distance = jnp.abs(freq) * 8
    for slot in range(slots):
        tile = assignment[slot]
        zone = zone_of[tile]
        keep = (distance < density[tile] * K).astype(jnp.float32)
        pupil = held[zone, 0:64, :].astype(jnp.float32).reshape(sources, 2, 8, K)
        start = pl.multiple_of(64 + 16 * (tile % 2), 16)
        mask = held[tile // 2, pl.ds(start, 16), :].astype(jnp.float32).reshape(2, 8, K) * keep
        real = pupil[:, 0] * mask[0] - pupil[:, 1] * mask[1]
        imag = pupil[:, 0] * mask[1] + pupil[:, 1] * mask[0]
        both = jnp.stack([real.reshape(2, 16, K), imag.reshape(2, 16, K)], 1).reshape(64, K)
        first = 64 * (slot % per_device)
        out[slot // per_device, first : first + 64, :] = both.astype(jnp.bfloat16)


def image_kernel(weights, products, columns, rows, out):
    stacked = []
    for piece in range(4):
        real = products[:, 32 * piece : 32 * piece + 16, :].reshape(2 * K, K)
        imag = products[:, 32 * piece + 16 : 32 * piece + 32, :].reshape(2 * K, K)
        stacked.append(jnp.concatenate([real, imag], 1))
    halves = jnp.dot(jnp.concatenate(stacked, 0), columns[...], preferred_element_type=jnp.float32)
    halves = halves.reshape(2, 2, K // 8, 2, 8, 2 * WIDE)
    images = []
    for slot in range(2):
        sides = []
        for source in range(4):
            half = halves[slot, source // 2, :, source % 2].reshape(K, 2 * WIDE).astype(jnp.bfloat16)
            sides.append(jnp.concatenate([half[:, :WIDE], half[:, WIDE:]], 0))
        field = jnp.dot(rows[slot], jnp.concatenate(sides, 1), preferred_element_type=jnp.float32)
        power = field[:ROWS] * field[:ROWS] + field[ROWS:] * field[ROWS:]
        total = jnp.zeros((ROWS, WIDE), jnp.float32)
        for source in range(4):
            total = total + weights[source].astype(jnp.float32) * power[:, source * WIDE : (source + 1) * WIDE]
        images.append(total)
    weight_sum = weights[0] + weights[1] + weights[2] + weights[3]
    last = lax.broadcasted_iota(jnp.int32, (ROWS, WIDE), 1) == SAMPLES
    even = lax.broadcasted_iota(jnp.int32, (ROWS, WIDE), 0) % 2 == 0
    first = jnp.where(last, weight_sum.astype(jnp.float32), images[0])
    second = jnp.where(last, weight_sum.astype(jnp.float32), images[1])
    lower = jnp.where(even, first, second).reshape(ROWS // 8, 8, WIDE)
    upper = jnp.where(even, pltpu.roll(first, ROWS - 1, 0), pltpu.roll(second, 1, 0)).reshape(ROWS // 8, 8, WIDE)
    out[...] = jnp.stack([lower, upper], 1).reshape(ROWS // 4, 8, WIDE).astype(out.dtype)


def finish_kernel(parts, table, out):
    summed = jnp.sum(parts[...].astype(jnp.float32), 0)
    total = summed[:, SAMPLES:]
    inside = lax.broadcasted_iota(jnp.int32, summed.shape, 1) < SAMPLES
    mean = jnp.sum(jnp.where(inside, summed, 0.0), 1, keepdims=True) * (1.0 / SAMPLES)
    rest = jnp.where(inside, summed - mean, 0.0)
    coarse = rest.astype(jnp.bfloat16)
    fine = (rest - coarse.astype(jnp.float32)).astype(jnp.bfloat16)
    both = jnp.concatenate([coarse, fine], 0)
    spread = jnp.dot(both, table[...], preferred_element_type=jnp.float32)
    result = (mean + (spread[:8] + spread[8:])) / total
    for row in range(out.shape[0]):
        out[row] = result[2 * row : 2 * row + 2]


def shards(spectra, pupils, zone_of, density, assignment, weights):
    devices = lax.axis_size("tile")
    sources = pupils.shape[1]
    scalars = pl.BlockSpec(memory_space=pltpu.SMEM)
    blocks = pl.BlockSpec(memory_space=pltpu.VMEM)
    params = pltpu.CompilerParams(vmem_limit_bytes=VMEM_LIMIT)

    hbm = pl.BlockSpec(memory_space=pltpu.HBM)
    tables = [assignment, zone_of, density, weights]
    laid, assignment, zone_of, density, weights = pl.pallas_call(
        layout_kernel,
        out_shape=[jax.ShapeDtypeStruct((devices, 12, 8, K), jnp.bfloat16)] + [pltpu.SMEM(x.shape, x.dtype) for x in tables],
        in_specs=[hbm] * 6,
        out_specs=[blocks] + [scalars] * 4,
        scratch_shapes=[pltpu.SemaphoreType.DMA((16,))],
        compiler_params=params,
        name="layout",
    )(
        pltpu.with_memory_space_constraint(pupils.reshape(sources, 2, devices, 8, K), pltpu.HBM),
        pltpu.with_memory_space_constraint(spectra.reshape(2, 2, devices, 8, K), pltpu.HBM),
        *(pltpu.with_memory_space_constraint(x, pltpu.HBM) for x in tables),
    )
    held = lax.all_to_all(laid.reshape(devices, 96, K), "tile", 0, 0, tiled=True)

    products = pl.pallas_call(
        product_kernel,
        out_shape=jax.ShapeDtypeStruct((devices, 2 * sources * 16, K), jnp.bfloat16),
        in_specs=[scalars] * 3 + [blocks],
        out_specs=blocks,
        compiler_params=params,
        name="products",
    )(assignment, zone_of, density, held)
    products = lax.all_to_all(products, "tile", 0, 0, tiled=True)

    image = pl.pallas_call(
        image_kernel,
        out_shape=jax.ShapeDtypeStruct((ROWS // 4, 8, WIDE), jnp.bfloat16),
        in_specs=[scalars] + [blocks] * 3,
        out_specs=blocks,
        compiler_params=params,
        name="images",
    )(weights, products, jnp.asarray(sample_table()), jnp.asarray(row_tables()))
    parts = lax.all_to_all(image, "src", 0, 0, tiled=True)

    return pl.pallas_call(
        finish_kernel,
        out_shape=jax.ShapeDtypeStruct((4, 2, NPIX), jnp.float32),
        in_specs=[blocks] * 2,
        out_specs=blocks,
        compiler_params=params,
        name="finish",
    )(parts, jnp.asarray(interpolation_table()))


def solution(mesh):
    return jax.shard_map(
        shards,
        mesh=mesh,
        in_specs=(
            P("tile", None, None, None),
            P("tile", "src", None, None, None),
            P(),
            P(),
            P(),
            P("src"),
        ),
        out_specs=P("src", "tile", None),
        check_vma=False,
    )
```
